256 devices in a mesh: seq: 16 (over y, x), mp: 8 (over z), dp: 2 (over core).
Axes of the slice: x: 4, y: 4, z: 8, core: 2. Of those that a mesh axis runs over, the one named last changes fastest.
Arguments:
- queries: bfloat16 [2, 4096, 4096], P('dp', 'seq', 'mp'), may hold values from -8 to 8
- encodings: bfloat16 [2, 2, 256, 128, 4096], P('dp', None, 'seq', None, 'mp'), may hold values from -8 to 8
- sink: float32 [32], P('mp'), may hold values from 1 to 6
- owner: int32 [2, 128], P('dp'), may hold values from 0 to 15, as said below
- doc_start: int32 [2, 64], P('dp'), may hold values 0 or 1
- d_out: bfloat16 [2, 4096, 4096], P('dp', 'seq', 'mp'), may hold values from -8 to 8
Outputs:
- attended: bfloat16 [2, 4096, 4096], P('dp', 'seq', 'mp')
- d_queries: bfloat16 [2, 4096, 4096], P('dp', 'seq', 'mp')
- d_encodings: bfloat16 [2, 2, 256, 128, 4096], P('dp', None, 'seq', None, 'mp')
- d_sink: float32 [32], P('mp')
The draws below stay inside these ranges and needn't reach their ends.
Inputs may be any that keep to these rules, and one draw needn't show every extreme that they name: `owner`: neighbour n belongs to span n // 2. One encoder group holds at most 16 neighbours of a sample, and some group exactly 16; of the neighbours of any 4 consecutive spans at most 2 are held by one group, and exactly 2 in some aligned block of 4 spans.
All inputs are finite; a program needn't handle non-finite values. No bound on the sum of `doc_start` on one device may be relied on, other than what follows from the above.
Results may differ from the reference program's by a relative error of at most 0.011.
Values may be sent and summed in bfloat16 or wider, within the bound.
No kernel may reach another device: no remote copies, remote signals or barrier semaphores. Data moves between devices by JAX's collectives and lax.ppermute only.
A program may use at most 128 MiB of HBM per device.

```python
import math
import jax
import jax.numpy as jnp
from jax import lax

HEADS = 32
HD = 128
CH = 64
NB = 2
NL = 128
CPD = 4
HF = 4096
SEQ = 4096
SPANS = 64
NEIGH = 128
BATCH = 2
ENC_CAP = 16
ENC_SLOTS = 256
N_SEQ = 16


def draw_queries(key, part):
    key = jax.random.fold_in(key, 3)
    key_noise = jax.random.fold_in(key, 0)
    shape_full = (BATCH, SEQ, HF)
    gauss_part = jax.random.normal(key_noise, shape_full, jnp.float32)
    values = 2.0 * gauss_part
    return jnp.clip(values, -8.0, 8.0).astype(jnp.bfloat16)


def draw_encodings(key, part):
    key = jax.random.fold_in(key, 5)
    key_keys, key_values = jax.random.split(key, 2)
    half_shape = (BATCH, ENC_SLOTS, NL, HF)
    key_part = jax.random.normal(key_keys, half_shape, jnp.float32)
    key_rows = key_part
    value_rows = jax.random.normal(key_values, half_shape, jnp.float32)
    values = jnp.stack([key_rows, value_rows], axis=1)
    return jnp.clip(values, -8.0, 8.0).astype(jnp.bfloat16)


def draw_d_out(key, part):
    key = jax.random.fold_in(key, 7)
    key_noise = jax.random.fold_in(key, 0)
    shape_full = (BATCH, SEQ, HF)
    ramp_up = 1.0 + 2.0 * jnp.arange(SEQ, dtype=jnp.float32) / max(SEQ - 1, 1)
    ramp_up = ramp_up[None, :, None]
    values = ramp_up * jax.random.normal(key_noise, shape_full, jnp.float32)
    return jnp.clip(values, -8.0, 8.0).astype(jnp.bfloat16)


def lane_members(lane_key, chosen):
    rounds = NEIGH // CPD
    shuffled = jax.random.permutation(lane_key, rounds).astype(jnp.int32)
    round_ids = jnp.arange(rounds, dtype=jnp.int32)
    scoring = shuffled + jnp.where(round_ids // 2 == chosen, 0, rounds)
    ranking = jnp.argsort(jnp.argsort(scoring)).astype(jnp.int32)
    others = max(N_SEQ // CPD - 1, 1)
    return jnp.where(ranking < ENC_CAP, 0, 1 + (ranking - ENC_CAP) % others)


def sample_groups(row_key):
    lane_count = CPD
    rounds = NEIGH // CPD
    key_order, key_lanes, key_pick = jax.random.split(row_key, 3)
    enc_order = jax.random.permutation(key_order, N_SEQ).astype(jnp.int32)
    chosen = jax.random.randint(key_pick, (lane_count,), 0, rounds // 2)
    member = jax.vmap(lane_members)(jax.random.split(key_lanes, lane_count), chosen)
    groups = jnp.take(enc_order, jnp.arange(lane_count, dtype=jnp.int32)[:, None] + lane_count * member)
    return groups.T.reshape(NEIGH)


def draw_owner(key, part):
    key = jax.random.fold_in(key, 11)
    return jax.vmap(sample_groups)(jax.random.split(key, BATCH)).astype(jnp.int32)


def with_ends(array, own_key, least, high):
    shape = array.shape
    index_at = [jax.random.randint(jax.random.fold_in(own_key, axis), (), 0, shape[axis]) for axis in range(len(shape))]
    array = array.at[tuple(index_at)].set(least)
    longest = shape.index(max(shape))
    index_at[longest] = (index_at[longest] + 1) % shape[longest]
    return array.at[tuple(index_at)].set(high)


def shard_levels(own_key, dims, cuts, least, top_value):
    def one(position, shards_of):
        steps = jax.random.uniform(jax.random.fold_in(jax.random.fold_in(own_key, 6), position), (shards_of,), jnp.float32, least / len(cuts), top_value / len(cuts))
        return jnp.repeat(jnp.exp(steps), dims[position] // shards_of).reshape((-1,) + (1,) * (len(dims) - position - 1))

    loudness = one(*cuts[0])
    for cut in cuts[1:]:
        loudness = loudness * one(*cut)
    return loudness


def setup_inputs(seed: int = 0) -> dict:
    splits = jax.random.split(jax.random.key(seed), 7)
    queries = draw_queries(jax.random.fold_in(splits[6], 71), 0)
    encodings = draw_encodings(jax.random.fold_in(splits[6], 71), 0)
    sink = jnp.clip(1.0 + 5.0 * jax.random.uniform(splits[2], (HEADS,), jnp.float32) ** shard_levels(splits[2], (HEADS,), ((0, 8),), -0.2, 0.2), 1.0, 6.0)
    owner = draw_owner(jax.random.fold_in(splits[6], 71), 0)
    doc_start = with_ends((jax.random.randint(splits[4], (BATCH, SPANS), 0, 6) < 1).astype(jnp.int32), jax.random.fold_in(splits[4], 1), 0, 1)
    d_out = draw_d_out(jax.random.fold_in(splits[6], 71), 0)
    return {"queries": queries, "encodings": encodings, "sink": sink, "owner": owner, "doc_start": doc_start, "d_out": d_out}


def block_step(query_blk, key_blk, value_blk, grad_blk, sink, is_live):
    scores = jnp.einsum('cqhd,ckhd->chqk', query_blk.astype(jnp.float32), key_blk.astype(jnp.float32)) * (HD ** -0.5)
    floor_logit = jnp.broadcast_to(sink[None, :, None], scores.shape[:3])
    live_rows = is_live[:, None, None]
    largest = jnp.where(live_rows, jnp.maximum(jnp.max(scores, axis=-1), floor_logit), floor_logit)
    powers = jnp.where(live_rows[..., None], jnp.exp(scores - largest[..., None]), 0.0)
    totals = jnp.exp(floor_logit - largest) + jnp.sum(powers, axis=-1)
    weights = powers / totals[..., None]
    low_weights = lax.optimization_barrier(weights.astype(jnp.bfloat16)).astype(jnp.float32)
    values_wide = value_blk.astype(jnp.float32)
    grads_wide = grad_blk.astype(jnp.float32)
    context = jnp.einsum('chqk,ckhd->cqhd', low_weights, values_wide)
    d_weights = jnp.einsum('cqhd,ckhd->chqk', grads_wide, values_wide)
    deltas = jnp.einsum('cqhd,cqhd->chq', grads_wide, context)
    d_scores = (weights * (d_weights - deltas[..., None]) * (HD ** -0.5)).astype(jnp.bfloat16)
    d_scores = lax.optimization_barrier(d_scores).astype(jnp.float32)
    grad_query = jnp.einsum('chqk,ckhd->cqhd', d_scores, key_blk.astype(jnp.float32))
    grad_key = jnp.einsum('chqk,cqhd->ckhd', d_scores, query_blk.astype(jnp.float32))
    grad_value = jnp.einsum('chqk,cqhd->ckhd', low_weights, grads_wide)
    sink_part = -jnp.sum(jnp.exp(floor_logit - largest) / totals * deltas, axis=(0, 2))
    return (context.astype(jnp.bfloat16), grad_query.astype(jnp.bfloat16), grad_key.astype(jnp.bfloat16), grad_value.astype(jnp.bfloat16), sink_part)


def one_sample(query_rows, enc_slots, owner_row, doc_row, grad_rows, sink):
    neigh_ids = jnp.arange(NEIGH, dtype=jnp.int32)
    before = neigh_ids[None, :] < neigh_ids[:, None]
    same_group = owner_row[None, :] == owner_row[:, None]
    slot_of = jnp.sum(before & same_group, axis=1).astype(jnp.int32)
    slot_rows = owner_row.astype(jnp.int32) * ENC_CAP + slot_of
    neigh_keys = jnp.take(enc_slots[0], slot_rows, axis=0).reshape(SPANS, NB * NL, HEADS, HD)
    neigh_values = jnp.take(enc_slots[1], slot_rows, axis=0).reshape(SPANS, NB * NL, HEADS, HD)
    prev_keys = jnp.concatenate([jnp.zeros_like(neigh_keys[:1]), neigh_keys[:-1]], axis=0)
    prev_values = jnp.concatenate([jnp.zeros_like(neigh_values[:1]), neigh_values[:-1]], axis=0)
    is_live = (jnp.arange(SPANS, dtype=jnp.int32) >= 1) & (doc_row == 0)
    group_size = math.gcd(SPANS, 8)
    blocks = SPANS // group_size

    def grouped(tensor):
        return tensor.reshape((blocks, group_size) + tensor.shape[1:])

    def run_block(pieces):
        return block_step(pieces[0], pieces[1], pieces[2], pieces[3], sink, pieces[4])

    outputs = lax.map(run_block, (grouped(query_rows.reshape(SPANS, CH, HEADS, HD)), grouped(prev_keys), grouped(prev_values), grouped(grad_rows.reshape(SPANS, CH, HEADS, HD)), grouped(is_live)))
    attended = outputs[0].reshape(SEQ, HF)
    grad_query = outputs[1].reshape(SEQ, HF)
    grad_key = outputs[2].reshape(SPANS, NB * NL * HF)
    grad_key = jnp.concatenate([grad_key[1:], jnp.zeros_like(grad_key[:1])], axis=0).reshape(NEIGH, NL, HF)
    grad_value = outputs[3].reshape(SPANS, NB * NL * HF)
    grad_value = jnp.concatenate([grad_value[1:], jnp.zeros_like(grad_value[:1])], axis=0).reshape(NEIGH, NL, HF)
    enc_grads = jnp.zeros((2, ENC_SLOTS, NL, HF), jnp.bfloat16)
    enc_grads = enc_grads.at[0, slot_rows].set(grad_key).at[1, slot_rows].set(grad_value)
    return attended, grad_query, enc_grads, jnp.sum(outputs[4], axis=0)


def reference(queries, encodings, sink, owner, doc_start, d_out):
    def per_sample(pieces):
        return one_sample(pieces[0], pieces[1], pieces[2], pieces[3], pieces[4], sink)

    results = lax.map(per_sample, (queries, encodings, owner, doc_start, d_out))
    return (results[0], results[1], results[2], jnp.sum(results[3], axis=0))
```

```python
import functools

import jax
import jax.numpy as jnp
from jax import lax
from jax.experimental import pallas as pl
from jax.experimental.pallas import tpu as pltpu
from jax.sharding import PartitionSpec as P

HD = 128
CH = 64
NB = 2
NL = 128
HALF = CH // 2
SCALE = HD ** (-0.5)
VMEM = 56 * 1024 * 1024
SLOT_STEP = 4


def params():
    return pltpu.CompilerParams(vmem_limit_bytes=VMEM)


def cost(flops, data):
    return pl.CostEstimate(flops=flops, bytes_accessed=data, transcendentals=0)


def cut_stripes(query_ref, grad_ref, out_ref):
    spans, heads = out_ref.shape[1], query_ref.shape[1] // HD
    for which, ref in enumerate((query_ref, grad_ref)):
        for head in range(heads):
            for half in range(2):
                stripe = (which * heads + head) * 2 + half
                for span in range(spans):
                    row = span * CH + half * HALF
                    out_ref[stripe, span] = ref[row : row + HALF, head * HD : (head + 1) * HD]


def join_stripes(in_ref, attended_ref, query_ref):
    spans, heads = in_ref.shape[1], attended_ref.shape[1] // HD
    for which, ref in enumerate((attended_ref, query_ref)):
        for head in range(heads):
            for half in range(2):
                stripe = (which * heads + head) * 2 + half
                for span in range(spans):
                    row = span * CH + half * HALF
                    ref[row : row + HALF, head * HD : (head + 1) * HD] = in_ref[stripe, span]


def spread_spans(meta_ref, in_ref, out_ref):
    count = out_ref.shape[0]
    first = pl.program_id(0) * count

    def body(i, carry):
        out_ref[i] = in_ref[meta_ref[first + i] & 63]
        return carry

    lax.fori_loop(0, count, body, 0, unroll=8)


def add_partials(meta_ref, in_ref, out_ref, *, pos_at):
    def body(span, carry):
        here = pos_at + 2 * span - NB
        left = in_ref[meta_ref[here]].astype(jnp.float32)
        right = in_ref[meta_ref[here + 1]].astype(jnp.float32)
        out_ref[span] = (left + right).astype(jnp.bfloat16)
        return carry

    out_ref[0] = jnp.zeros(out_ref.shape[1:], jnp.bfloat16)
    lax.fori_loop(1, out_ref.shape[0], body, 0, unroll=7)


def paired(stripes_ref, which, pair, slot, heads):
    nothing = jnp.zeros((CH, HD), jnp.bfloat16)
    blocks = []
    for head in (2 * pair, 2 * pair + 1):
        at = (which * heads + head) * 2
        blocks.append(jnp.concatenate([stripes_ref[at, slot], stripes_ref[at + 1, slot]], axis=0))
    return jnp.concatenate(
        [
            jnp.concatenate([blocks[0], nothing], axis=1),
            jnp.concatenate([nothing, blocks[1]], axis=1),
        ],
        axis=0,
    )


def dot(left, right, left_dim, right_dim):
    return lax.dot_general(
        left, right, (((left_dim,), (right_dim,)), ((), ())), preferred_element_type=jnp.float32
    )


def stats_of(stripes_ref, enc_ref, out_ref):
    heads = enc_ref.shape[3] // HD
    pairs = heads // 2
    for slot in range(enc_ref.shape[1]):
        for pair in range(pairs):
            cols = slice(pair * 2 * HD, (pair + 1) * 2 * HD)
            queries = paired(stripes_ref, 0, pair, slot, heads)
            grads = paired(stripes_ref, 1, pair, slot, heads)
            scores = dot(enc_ref[0, slot, :, cols], queries, 1, 1) * SCALE
            d_weights = dot(enc_ref[1, slot, :, cols], grads, 1, 1)
            top = jnp.max(scores, axis=0, keepdims=True)
            powers = jnp.exp(scores - top)
            total = jnp.sum(powers, axis=0, keepdims=True)
            delta = jnp.sum(powers * d_weights, axis=0, keepdims=True) / total
            log_total = top + jnp.log(total)
            for dest in range(out_ref.shape[0]):
                out_ref[dest, slot, pair : pair + 1] = log_total
                out_ref[dest, slot, pairs + pair : pairs + pair + 1] = delta


def joined(mine, other, sink):
    pairs = sink.shape[0]
    log_a, log_b = mine[:pairs], other[:pairs]
    top = jnp.maximum(jnp.maximum(log_a, log_b), sink)
    part_a, part_b, part_s = jnp.exp(log_a - top), jnp.exp(log_b - top), jnp.exp(sink - top)
    total = part_a + part_b + part_s
    deltas = (part_a * mine[pairs:] + part_b * other[pairs:]) / total
    return top + jnp.log(total), deltas, part_s / total


def slot_terms(meta_ref, stripes_ref, enc_ref, stats_ref, sink_ref, slot, me_at):
    heads = enc_ref.shape[3] // HD
    here = pl.program_id(0) * enc_ref.shape[1] + slot
    mine_at = meta_ref[me_at] + here
    code = meta_ref[mine_at]
    live = ((code >> 6) & 1).astype(jnp.float32)
    log_total, deltas, _ = joined(stats_ref[mine_at], stats_ref[code >> 7], sink_ref[...])
    for pair in range(heads // 2):
        cols = slice(pair * 2 * HD, (pair + 1) * 2 * HD)
        queries = paired(stripes_ref, 0, pair, slot, heads)
        grads = paired(stripes_ref, 1, pair, slot, heads)
        keys, values = enc_ref[0, slot, :, cols], enc_ref[1, slot, :, cols]
        scores = dot(keys, queries, 1, 1) * SCALE
        d_weights = dot(values, grads, 1, 1)
        weights = jnp.exp(scores - log_total[pair : pair + 1]) * live
        d_scores = (weights * (d_weights - deltas[pair : pair + 1]) * SCALE).astype(jnp.bfloat16)
        yield pair, cols, queries, grads, keys, values, weights.astype(jnp.bfloat16), d_scores


def token_side(meta_ref, stripes_ref, enc_ref, stats_ref, sink_ref, out_ref, *, me_at):
    heads = enc_ref.shape[3] // HD
    for slot in range(enc_ref.shape[1]):
        for pair, _, _, _, keys, values, weights, d_scores in slot_terms(
            meta_ref, stripes_ref, enc_ref, stats_ref, sink_ref, slot, me_at
        ):
            for which, (left, right) in enumerate(((weights, values), (d_scores, keys))):
                rows = dot(left, right, 0, 0).astype(jnp.bfloat16)
                for side in range(2):
                    for half in range(2):
                        stripe = (which * heads + 2 * pair + side) * 2 + half
                        at = side * CH + half * HALF
                        out_ref[stripe, slot] = rows[at : at + HALF, side * HD : (side + 1) * HD]


def slot_side(meta_ref, stripes_ref, enc_ref, stats_ref, sink_ref, out_ref, *, me_at):
    for slot in range(enc_ref.shape[1]):
        for _, cols, queries, grads, _, _, weights, d_scores in slot_terms(
            meta_ref, stripes_ref, enc_ref, stats_ref, sink_ref, slot, me_at
        ):
            out_ref[0, slot, :, cols] = dot(d_scores, queries, 1, 0).astype(jnp.bfloat16)
            out_ref[1, slot, :, cols] = dot(weights, grads, 1, 0).astype(jnp.bfloat16)


def sink_side(meta_ref, stats_ref, sink_ref, out_ref, *, pos_at, live_at, spans):
    sink = sink_ref[...]

    def body(span, total):
        here = pos_at + 2 * span - NB
        live = meta_ref[live_at + span].astype(jnp.float32)
        _, deltas, part = joined(stats_ref[meta_ref[here]], stats_ref[meta_ref[here + 1]], sink)
        return total - part * deltas * live

    out_ref[...] = lax.fori_loop(1, spans, body, jnp.zeros_like(sink), unroll=7)


def routing(owner_row, doc_row, seq_index, slots, seq_count):
    neigh_count, spans = owner_row.shape[0], doc_row.shape[0]
    neigh_ids = jnp.arange(neigh_count, dtype=jnp.int32)
    before = neigh_ids[None, :] < neigh_ids[:, None]
    same_owner = owner_row[None, :] == owner_row[:, None]
    slot_of = jnp.sum(before & same_owner, axis=1).astype(jnp.int32)
    place = owner_row * slots + slot_of
    other = jnp.flip(place.reshape(spans, NB), axis=1).reshape(-1)
    span_ids = jnp.arange(spans, dtype=jnp.int32)
    live = ((span_ids >= 1) & (doc_row == 0)).astype(jnp.int32)
    next_live = jnp.concatenate([live[1:], jnp.zeros((1,), jnp.int32)])
    reader = jnp.minimum(neigh_ids // NB + 1, spans - 1)
    code = reader + 64 * jnp.repeat(next_live, NB) + 128 * other
    flat = jnp.arange(slots * seq_count, dtype=jnp.int32)
    codes = jnp.sum(jnp.where(place[None, :] == flat[:, None], code[None, :], 0), axis=1)
    first = (seq_index * slots).astype(jnp.int32).reshape(1)
    return jnp.concatenate([codes, place, live, first])


def on_device(queries, encodings, sink, owner, doc_start, d_out):
    seq_count = lax.axis_size("seq")
    seq_index = lax.axis_index("seq")
    tokens, width = queries.shape[1:]
    spans_here = tokens // CH
    heads = width // HD
    pairs = heads // 2
    slots = encodings.shape[2]
    spans, neighs = doc_start.shape[1], owner.shape[1]
    places = seq_count * slots
    pos_at = places
    live_at = pos_at + neighs
    me_at = live_at + spans
    bf16 = jnp.bfloat16
    f32 = jnp.float32

    meta = routing(owner[0], doc_start[0], seq_index, slots, seq_count)
    sink_rows = jnp.repeat(sink.reshape(pairs, 2), CH, axis=1)

    def everywhere(block):
        return lax.all_to_all(block, "seq", split_axis=0, concat_axis=0, tiled=True)

    stripe = (HALF, HD)
    cut = pl.pallas_call(
        cut_stripes,
        out_shape=jax.ShapeDtypeStruct((seq_count, spans_here) + stripe, bf16),
        compiler_params=params(),
        name="cut_stripes",
    )(queries[0], d_out[0])
    all_spans = everywhere(cut).reshape((spans,) + stripe)

    per = places // 4
    spread = pl.pallas_call(
        spread_spans,
        grid_spec=pltpu.PrefetchScalarGridSpec(
            num_scalar_prefetch=1,
            grid=(4,),
            in_specs=[pl.BlockSpec((spans,) + stripe, lambda i, m: (0, 0, 0))],
            out_specs=pl.BlockSpec((per,) + stripe, lambda i, m: (i, 0, 0)),
        ),
        out_shape=jax.ShapeDtypeStruct((places,) + stripe, bf16),
        compiler_params=params(),
        name="spread_spans",
    )(meta, all_spans)
    stripes = everywhere(spread.reshape((seq_count, slots) + stripe))

    enc = encodings[0]
    grid = (slots // SLOT_STEP,)
    stripes_block = (seq_count, SLOT_STEP) + stripe
    enc_block = (2, SLOT_STEP, NL, width)
    one_dot = 2 * NL * CH * width * slots
    stats = pl.pallas_call(
        stats_of,
        grid=grid,
        in_specs=[
            pl.BlockSpec(stripes_block, lambda i: (0, i, 0, 0)),
            pl.BlockSpec(enc_block, lambda i: (0, i, 0, 0)),
        ],
        out_specs=pl.BlockSpec((seq_count, SLOT_STEP, heads, HD), lambda i: (0, i, 0, 0)),
        out_shape=jax.ShapeDtypeStruct((seq_count, slots, heads, HD), f32),
        compiler_params=params(),
        cost_estimate=cost(2 * one_dot, stripes.size * 2 + enc.size * 2),
        name="stats",
    )(stripes, enc)
    all_stats = everywhere(stats).reshape(places, heads, HD)

    def with_stats(kernel, out_block, out_shape, name):
        return pl.pallas_call(
            functools.partial(kernel, me_at=me_at),
            grid_spec=pltpu.PrefetchScalarGridSpec(
                num_scalar_prefetch=1,
                grid=grid,
                in_specs=[
                    pl.BlockSpec(stripes_block, lambda i, m: (0, i, 0, 0)),
                    pl.BlockSpec(enc_block, lambda i, m: (0, i, 0, 0)),
                    pl.BlockSpec((places, heads, HD), lambda i, m: (0, 0, 0)),
                    pl.BlockSpec((pairs, HD), lambda i, m: (0, 0)),
                ],
                out_specs=pl.BlockSpec(out_block, lambda i, m: (0, i, 0, 0)),
            ),
            out_shape=jax.ShapeDtypeStruct(out_shape, bf16),
            compiler_params=params(),
            cost_estimate=cost(4 * one_dot, stripes.size * 2 + enc.size * 4),
            name=name,
        )(meta, stripes, enc, all_stats, sink_rows)

    partials = with_stats(token_side, stripes_block, stripes.shape, "token_side")
    returned = everywhere(partials).reshape((places,) + stripe)
    enc_grads = with_stats(slot_side, enc_block, enc.shape, "slot_side")

    sink_lanes = pl.pallas_call(
        functools.partial(sink_side, pos_at=pos_at, live_at=live_at, spans=spans),
        grid_spec=pltpu.PrefetchScalarGridSpec(
            num_scalar_prefetch=1,
            grid=(1,),
            in_specs=[
                pl.BlockSpec((places, heads, HD), lambda i, m: (0, 0, 0)),
                pl.BlockSpec((pairs, HD), lambda i, m: (0, 0)),
            ],
            out_specs=pl.BlockSpec((pairs, HD), lambda i, m: (0, 0)),
        ),
        out_shape=jax.ShapeDtypeStruct((pairs, HD), f32),
        compiler_params=params(),
        cost_estimate=cost(spans * 4096, all_stats.size * 4),
        name="sink_side",
    )(meta, all_stats, sink_rows)
    sink_part = jnp.sum(sink_lanes.reshape(heads, CH), axis=1)
    sink_total = sink_part + lax.ppermute(sink_part, "dp", [(0, 1), (1, 0)])

    summed = pl.pallas_call(
        functools.partial(add_partials, pos_at=pos_at),
        grid_spec=pltpu.PrefetchScalarGridSpec(
            num_scalar_prefetch=1,
            grid=(1,),
            in_specs=[pl.BlockSpec((places,) + stripe, lambda i, m: (0, 0, 0))],
            out_specs=pl.BlockSpec((spans,) + stripe, lambda i, m: (0, 0, 0)),
        ),
        out_shape=jax.ShapeDtypeStruct((spans,) + stripe, bf16),
        compiler_params=params(),
        name="add_partials",
    )(meta, returned)
    final = everywhere(summed.reshape((seq_count, spans_here) + stripe))
    attended, grad_query = pl.pallas_call(
        join_stripes,
        out_shape=[jax.ShapeDtypeStruct((tokens, width), bf16)] * 2,
        compiler_params=params(),
        name="join_stripes",
    )(final)
    return attended[None], grad_query[None], enc_grads[None], sink_total


def solution(mesh):
    in_specs = (
        P("dp", "seq", "mp"),
        P("dp", None, "seq", None, "mp"),
        P("mp"),
        P("dp", None),
        P("dp", None),
        P("dp", "seq", "mp"),
    )
    out_specs = (
        P("dp", "seq", "mp"),
        P("dp", "seq", "mp"),
        P("dp", None, "seq", None, "mp"),
        P("mp"),
    )
    return jax.shard_map(
        on_device, mesh=mesh, in_specs=in_specs, out_specs=out_specs, check_vma=False
    )
```

```python
import functools

import jax
import jax.numpy as jnp
from jax import lax
from jax.experimental import pallas as pl
from jax.experimental.pallas import tpu as pltpu
from jax.sharding import PartitionSpec as P

HD = 128
CH = 64
NB = 2
NL = 128
HALF = CH // 2
SCALE = HD ** (-0.5)
MIB = 1024 * 1024
GRAD_STEPS = 4
IN_VMEM = pl.BlockSpec(memory_space=pltpu.VMEM)
IN_SMEM = pl.BlockSpec(memory_space=pltpu.SMEM)


def cut_stripes(query_ref, grad_ref, out_ref):
    spans, heads = out_ref.shape[1], query_ref.shape[1] // HD
    for which, ref in enumerate((query_ref, grad_ref)):
        for head in range(heads):
            for half in range(2):
                stripe = (which * heads + head) * 2 + half
                for span in range(spans):
                    row = span * CH + half * HALF
                    out_ref[stripe, span] = ref[row : row + HALF, head * HD : (head + 1) * HD]


def join_stripes(in_ref, attended_ref, query_ref):
    spans, heads = in_ref.shape[1], attended_ref.shape[1] // HD
    for which, ref in enumerate((attended_ref, query_ref)):
        for head in range(heads):
            for half in range(2):
                stripe = (which * heads + head) * 2 + half
                for span in range(spans):
                    row = span * CH + half * HALF
                    ref[row : row + HALF, head * HD : (head + 1) * HD] = in_ref[stripe, span]


def spread_spans(meta_ref, in_ref, out_ref):
    def body(i, carry):
        out_ref[i] = in_ref[meta_ref[i] & 63]
        return carry

    lax.fori_loop(0, out_ref.shape[0], body, 0, unroll=16)


def add_partials(meta_ref, in_ref, out_ref, *, pos_at):
    def body(span, carry):
        here = pos_at + 2 * span - NB
        left = in_ref[meta_ref[here]].astype(jnp.float32)
        right = in_ref[meta_ref[here + 1]].astype(jnp.float32)
        out_ref[span] = (left + right).astype(jnp.bfloat16)
        return carry

    out_ref[0] = jnp.zeros(out_ref.shape[1:], jnp.bfloat16)
    lax.fori_loop(1, out_ref.shape[0], body, 0, unroll=9)


def paired(stripes_ref, which, pair, slot, heads):
    nothing = jnp.zeros((CH, HD), jnp.bfloat16)
    blocks = []
    for head in (2 * pair, 2 * pair + 1):
        at = (which * heads + head) * 2
        blocks.append(jnp.concatenate([stripes_ref[at, slot], stripes_ref[at + 1, slot]], axis=0))
    return jnp.concatenate(
        [
            jnp.concatenate([blocks[0], nothing], axis=1),
            jnp.concatenate([nothing, blocks[1]], axis=1),
        ],
        axis=0,
    )


def dot(left, right, left_dim, right_dim):
    return lax.dot_general(
        left, right, (((left_dim,), (right_dim,)), ((), ())), preferred_element_type=jnp.float32
    )


def stats_of(stripes_ref, enc_ref, out_ref):
    heads = enc_ref.shape[3] // HD
    pairs = heads // 2
    for slot in range(enc_ref.shape[1]):
        for pair in range(pairs):
            cols = slice(pair * 2 * HD, (pair + 1) * 2 * HD)
            queries = paired(stripes_ref, 0, pair, slot, heads)
            grads = paired(stripes_ref, 1, pair, slot, heads)
            scores = dot(enc_ref[0, slot, :, cols], queries, 1, 1) * SCALE
            d_weights = dot(enc_ref[1, slot, :, cols], grads, 1, 1)
            top = jnp.max(scores, axis=0, keepdims=True)
            powers = jnp.exp(scores - top)
            total = jnp.sum(powers, axis=0, keepdims=True)
            out_ref[0, slot, pair : pair + 1] = top + jnp.log(total)
            delta = jnp.sum(powers * d_weights, axis=0, keepdims=True) / total
            out_ref[0, slot, pairs + pair : pairs + pair + 1] = delta
    for dest in range(1, out_ref.shape[0]):
        out_ref[dest] = out_ref[0]


def joined(mine, other, sink):
    pairs = sink.shape[0]
    log_a, log_b = mine[:pairs], other[:pairs]
    top = jnp.maximum(jnp.maximum(log_a, log_b), sink)
    part_a, part_b, part_s = jnp.exp(log_a - top), jnp.exp(log_b - top), jnp.exp(sink - top)
    total = part_a + part_b + part_s
    deltas = (part_a * mine[pairs:] + part_b * other[pairs:]) / total
    return top + jnp.log(total), deltas, part_s / total


def slot_stats(meta_ref, stats_ref, sink_ref, slot, me_at):
    mine_at = meta_ref[me_at] + slot
    code = meta_ref[mine_at]
    live = ((code >> 6) & 1).astype(jnp.float32)
    log_total, deltas, _ = joined(stats_ref[mine_at], stats_ref[code >> 7], sink_ref[...])
    return log_total, deltas, live


def token_side(
    meta_ref, stripes_ref, enc_ref, stats_ref, sink_ref, out_ref, weights_ref, scores_ref, *, me_at
):
    heads = enc_ref.shape[3] // HD
    pairs = heads // 2
    slots = enc_ref.shape[1]
    for slot in range(slots):
        log_total, deltas, live = slot_stats(meta_ref, stats_ref, sink_ref, slot, me_at)
        spare = jnp.zeros((8 - 2 * pairs, 2 * CH), jnp.float32)
        columns = jnp.concatenate([log_total, deltas, spare], axis=0).T
        for pair in range(pairs):
            cols = slice(pair * 2 * HD, (pair + 1) * 2 * HD)
            queries = paired(stripes_ref, 0, pair, slot, heads)
            grads = paired(stripes_ref, 1, pair, slot, heads)
            scores = dot(queries, enc_ref[0, slot, :, cols], 1, 1) * SCALE
            d_weights = dot(grads, enc_ref[1, slot, :, cols], 1, 1)
            weights = jnp.exp(scores - columns[:, pair : pair + 1]) * live
            d_scores = weights * (d_weights - columns[:, pairs + pair : pairs + pair + 1]) * SCALE
            weights_ref[slot * pairs + pair] = weights.astype(jnp.bfloat16)
            scores_ref[slot * pairs + pair] = d_scores.astype(jnp.bfloat16)
    for slot in range(slots):
        for pair in range(pairs):
            cols = slice(pair * 2 * HD, (pair + 1) * 2 * HD)
            for which, ref in enumerate((weights_ref, scores_ref)):
                right = enc_ref[1 - which, slot, :, cols]
                rows = dot(ref[slot * pairs + pair], right, 1, 0).astype(jnp.bfloat16)
                for side in range(2):
                    for half in range(2):
                        stripe = (which * heads + 2 * pair + side) * 2 + half
                        at = side * CH + half * HALF
                        out_ref[stripe, slot] = rows[at : at + HALF, side * HD : (side + 1) * HD]


def slot_side(
    meta_ref, stripes_ref, enc_ref, stats_ref, sink_ref, out_ref, weights_ref, scores_ref, *, me_at
):
    heads = enc_ref.shape[3] // HD
    pairs = heads // 2
    count = out_ref.shape[1]
    first = pl.program_id(0) * count
    for step in range(count):
        slot = first + step
        log_total, deltas, live = slot_stats(meta_ref, stats_ref, sink_ref, slot, me_at)
        for pair in range(pairs):
            cols = slice(pair * 2 * HD, (pair + 1) * 2 * HD)
            queries = paired(stripes_ref, 0, pair, slot, heads)
            grads = paired(stripes_ref, 1, pair, slot, heads)
            scores = dot(enc_ref[0, slot, :, cols], queries, 1, 1) * SCALE
            d_weights = dot(enc_ref[1, slot, :, cols], grads, 1, 1)
            weights = jnp.exp(scores - log_total[pair : pair + 1]) * live
            d_scores = weights * (d_weights - deltas[pair : pair + 1]) * SCALE
            weights_ref[step * pairs + pair] = weights.astype(jnp.bfloat16)
            scores_ref[step * pairs + pair] = d_scores.astype(jnp.bfloat16)
    for step in range(count):
        slot = first + step
        for pair in range(pairs):
            cols = slice(pair * 2 * HD, (pair + 1) * 2 * HD)
            for which, ref in enumerate((scores_ref, weights_ref)):
                right = paired(stripes_ref, which, pair, slot, heads)
                rows = dot(ref[step * pairs + pair], right, 1, 0)
                out_ref[which, step, :, cols] = rows.astype(jnp.bfloat16)


def sink_side(meta_ref, stats_ref, sink_ref, out_ref, *, pos_at, live_at, spans):
    sink = sink_ref[...]

    def body(span, total):
        here = pos_at + 2 * span - NB
        live = meta_ref[live_at + span].astype(jnp.float32)
        _, deltas, part = joined(stats_ref[meta_ref[here]], stats_ref[meta_ref[here + 1]], sink)
        return total - part * deltas * live

    out_ref[...] = lax.fori_loop(1, spans, body, jnp.zeros_like(sink), unroll=7)


def routing(owner_row, doc_row, seq_index, slots, seq_count):
    neigh_count, spans = owner_row.shape[0], doc_row.shape[0]
    neigh_ids = jnp.arange(neigh_count, dtype=jnp.int32)
    before = neigh_ids[None, :] < neigh_ids[:, None]
    same_owner = owner_row[None, :] == owner_row[:, None]
    slot_of = jnp.sum(before & same_owner, axis=1).astype(jnp.int32)
    place = owner_row * slots + slot_of
    other = jnp.flip(place.reshape(spans, NB), axis=1).reshape(-1)
    span_ids = jnp.arange(spans, dtype=jnp.int32)
    live = ((span_ids >= 1) & (doc_row == 0)).astype(jnp.int32)
    next_live = jnp.concatenate([live[1:], jnp.zeros((1,), jnp.int32)])
    reader = jnp.minimum(neigh_ids // NB + 1, spans - 1)
    code = reader + 64 * jnp.repeat(next_live, NB) + 128 * other
    flat = jnp.arange(slots * seq_count, dtype=jnp.int32)
    codes = jnp.sum(jnp.where(place[None, :] == flat[:, None], code[None, :], 0), axis=1)
    first = (seq_index * slots).astype(jnp.int32).reshape(1)
    return jnp.concatenate([codes, place, live, first])


def on_device(queries, encodings, sink, owner, doc_start, d_out):
    seq_count = lax.axis_size("seq")
    seq_index = lax.axis_index("seq")
    tokens, width = queries.shape[1:]
    spans_here = tokens // CH
    heads = width // HD
    pairs = heads // 2
    slots = encodings.shape[2]
    spans, neighs = doc_start.shape[1], owner.shape[1]
    places = seq_count * slots
    pos_at = places
    live_at = pos_at + neighs
    me_at = live_at + spans
    bf16 = jnp.bfloat16
    f32 = jnp.float32
    stripe = (HALF, HD)
    tile = pltpu.VMEM((slots * pairs, NL, NL), bf16)
    flops = 4 * NL * CH * width * slots

    def everywhere(block):
        return lax.all_to_all(block, "seq", split_axis=0, concat_axis=0, tiled=True)

    def call(kernel, name, out, *operands, grid=(), out_specs=IN_VMEM, limit=16, work=0, **kw):
        return pl.pallas_call(
            kernel,
            grid=grid,
            in_specs=[IN_SMEM if x.dtype == jnp.int32 else IN_VMEM for x in operands],
            out_specs=out_specs,
            out_shape=out,
            compiler_params=pltpu.CompilerParams(vmem_limit_bytes=limit * MIB),
            cost_estimate=pl.CostEstimate(
                flops=work, bytes_accessed=sum(x.nbytes for x in operands), transcendentals=0
            ),
            name=name,
            **kw,
        )(*operands)

    meta = routing(owner[0], doc_start[0], seq_index, slots, seq_count)
    sink_rows = jnp.repeat(sink.reshape(pairs, 2), CH, axis=1)
    enc = encodings[0]

    def struct(shape, dtype=bf16):
        return jax.ShapeDtypeStruct(shape, dtype)

    cut = call(cut_stripes, "cut", struct((seq_count, spans_here) + stripe), queries[0], d_out[0])
    all_spans = everywhere(cut).reshape((spans,) + stripe)
    spread = call(spread_spans, "spread", struct((places,) + stripe), meta, all_spans)
    stripes = everywhere(spread.reshape((seq_count, slots) + stripe))
    stats = call(
        stats_of, "stats", struct((seq_count, slots, heads, HD), f32), stripes, enc, work=flops
    )
    all_stats = everywhere(stats).reshape(places, heads, HD)
    whole = (meta, stripes, enc, all_stats, sink_rows)
    partials = call(
        functools.partial(token_side, me_at=me_at),
        "token_side",
        struct(stripes.shape),
        *whole,
        work=2 * flops,
        scratch_shapes=[tile, tile],
    )
    returned = everywhere(partials).reshape((places,) + stripe)
    step = slots // GRAD_STEPS
    enc_grads = call(
        functools.partial(slot_side, me_at=me_at),
        "slot_side",
        struct(enc.shape),
        *whole,
        grid=(GRAD_STEPS,),
        out_specs=pl.BlockSpec((2, step, NL, width), lambda i: (0, i, 0, 0)),
        work=2 * flops,
        scratch_shapes=[pltpu.VMEM((step * pairs, NL, NL), bf16)] * 2,
    )
    sink_lanes = call(
        functools.partial(sink_side, pos_at=pos_at, live_at=live_at, spans=spans),
        "sink_side",
        struct((pairs, HD), f32),
        meta,
        all_stats,
        sink_rows,
        work=spans * 4096,
    )
    sink_part = jnp.sum(sink_lanes.reshape(heads, CH), axis=1)
    sink_total = sink_part + lax.ppermute(sink_part, "dp", [(0, 1), (1, 0)])
    returned, enc_grads, sink_total = lax.optimization_barrier((returned, enc_grads, sink_total))

    summed = call(
        functools.partial(add_partials, pos_at=pos_at),
        "add_partials",
        struct((spans,) + stripe),
        meta,
        returned,
    )
    final = everywhere(summed.reshape((seq_count, spans_here) + stripe))
    rows = pl.BlockSpec((tokens, width), lambda: (0, 0))
    attended, grad_query = call(
        join_stripes, "join", [struct((tokens, width))] * 2, final, out_specs=[rows, rows]
    )
    return attended[None], grad_query[None], enc_grads[None], sink_total


def solution(mesh):
    in_specs = (
        P("dp", "seq", "mp"),
        P("dp", None, "seq", None, "mp"),
        P("mp"),
        P("dp", None),
        P("dp", None),
        P("dp", "seq", "mp"),
    )
    out_specs = (
        P("dp", "seq", "mp"),
        P("dp", "seq", "mp"),
        P("dp", None, "seq", None, "mp"),
        P("mp"),
    )
    return jax.shard_map(
        on_device, mesh=mesh, in_specs=in_specs, out_specs=out_specs, check_vma=False
    )
```

```python
import functools

import jax
import jax.numpy as jnp
from jax import lax
from jax.experimental import pallas as pl
from jax.experimental.pallas import tpu as pltpu
from jax.sharding import PartitionSpec as P

HD = 128
CH = 64
NB = 2
NL = 128
HALF = CH // 2
SCALE = HD ** (-0.5)
MIB = 1024 * 1024
STEPS = 2
IN_VMEM = pl.BlockSpec(memory_space=pltpu.VMEM)
IN_HBM = pl.BlockSpec(memory_space=pltpu.HBM)
IN_SMEM = pl.BlockSpec(memory_space=pltpu.SMEM)


def cut_stripes(query_hbm, grad_hbm, out_hbm, rows_ref, out_ref, in_sems, out_sems):
    whiches, heads, halves, spans = out_ref.shape[:4]
    loads, stores = [], []
    for which, ref in enumerate((query_hbm, grad_hbm)):
        loads.append(pltpu.make_async_copy(ref, rows_ref.at[which], in_sems.at[which]))
        stores.append(
            pltpu.make_async_copy(out_ref.at[which], out_hbm.at[which], out_sems.at[which])
        )
        loads[which].start()
    for which in range(whiches):
        loads[which].wait()
        for head in range(heads):
            for half in range(halves):
                for span in range(spans):
                    row = span * CH + half * HALF
                    out_ref[which, head, half, span] = rows_ref[
                        which, row : row + HALF, head * HD : (head + 1) * HD
                    ]
        stores[which].start()
    for store in stores:
        store.wait()


def join_stripes(in_ref, attended_ref, query_ref):
    spans, heads = in_ref.shape[1], attended_ref.shape[1] // HD
    for which, ref in enumerate((attended_ref, query_ref)):
        for head in range(heads):
            for half in range(2):
                stripe = (which * heads + head) * 2 + half
                for span in range(spans):
                    row = span * CH + half * HALF
                    ref[row : row + HALF, head * HD : (head + 1) * HD] = in_ref[stripe, span]


def spread_spans(meta_ref, in_ref, sink_ref, out_ref):
    def body(i, carry):
        out_ref[i] = in_ref[meta_ref[i] & 63]
        return carry

    lax.fori_loop(0, out_ref.shape[0], body, 0, unroll=16)


def add_partials(meta_ref, in_ref, out_ref, *, pos_at):

    def body(span, carry):
        here = pos_at + 2 * span - NB
        left = in_ref[meta_ref[here]].astype(jnp.float32)
        right = in_ref[meta_ref[here + 1]].astype(jnp.float32)
        out_ref[span] = (left + right).astype(jnp.bfloat16)
        return carry

    out_ref[0] = jnp.zeros(out_ref.shape[1:], jnp.bfloat16)
    lax.fori_loop(1, out_ref.shape[0], body, 0, unroll=9)


def paired(stripes_ref, which, pair, slot, heads):
    nothing = jnp.zeros((CH, HD), jnp.bfloat16)
    blocks = []
    for head in (2 * pair, 2 * pair + 1):
        at = (which * heads + head) * 2
        blocks.append(jnp.concatenate([stripes_ref[at, slot], stripes_ref[at + 1, slot]], axis=0))
    return jnp.concatenate(
        [
            jnp.concatenate([blocks[0], nothing], axis=1),
            jnp.concatenate([nothing, blocks[1]], axis=1),
        ],
        axis=0,
    )


def dot(left, right, left_dim, right_dim):
    return lax.dot_general(
        left, right, (((left_dim,), (right_dim,)), ((), ())), preferred_element_type=jnp.float32
    )


def stats_of(stripes_ref, enc_ref, out_ref):
    heads = enc_ref.shape[3] // HD
    pairs = heads // 2
    count = out_ref.shape[1]
    first = pl.program_id(0) * count
    for step in range(count):
        slot = first + step
        for pair in range(pairs):
            cols = slice(pair * 2 * HD, (pair + 1) * 2 * HD)
            queries = paired(stripes_ref, 0, pair, slot, heads)
            grads = paired(stripes_ref, 1, pair, slot, heads)
            scores = dot(enc_ref[0, slot, :, cols], queries, 1, 1) * SCALE
            d_weights = dot(enc_ref[1, slot, :, cols], grads, 1, 1)
            top = jnp.max(scores, axis=0, keepdims=True)
            powers = jnp.exp(scores - top)
            total = jnp.sum(powers, axis=0, keepdims=True)
            out_ref[0, step, pair : pair + 1] = top + jnp.log(total)
            delta = jnp.sum(powers * d_weights, axis=0, keepdims=True) / total
            out_ref[0, step, pairs + pair : pairs + pair + 1] = delta
    for dest in range(1, out_ref.shape[0]):
        out_ref[dest] = out_ref[0]


def joined(mine, other, sink):
    pairs = sink.shape[0]
    log_a, log_b = mine[:pairs], other[:pairs]
    top = jnp.maximum(jnp.maximum(log_a, log_b), sink)
    part_a, part_b, part_s = jnp.exp(log_a - top), jnp.exp(log_b - top), jnp.exp(sink - top)
    total = part_a + part_b + part_s
    deltas = (part_a * mine[pairs:] + part_b * other[pairs:]) / total
    return top + jnp.log(total), deltas, part_s / total


def slot_stats(meta_ref, stats_ref, sink_ref, slot, me_at):
    mine_at = meta_ref[me_at] + slot
    code = meta_ref[mine_at]
    live = ((code >> 6) & 1).astype(jnp.float32)
    log_total, deltas, _ = joined(stats_ref[mine_at], stats_ref[code >> 7], sink_ref[...])
    return log_total, deltas, live


def token_side(
    meta_ref, stripes_ref, enc_ref, stats_ref, sink_ref, out_ref, weights_ref, scores_ref, *, me_at
):
    heads = enc_ref.shape[3] // HD
    pairs = heads // 2
    slots = enc_ref.shape[1]
    for slot in range(slots):
        log_total, deltas, live = slot_stats(meta_ref, stats_ref, sink_ref, slot, me_at)
        spare = jnp.zeros((8 - 2 * pairs, 2 * CH), jnp.float32)
        columns = jnp.concatenate([log_total, deltas, spare], axis=0).T
        for pair in range(pairs):
            cols = slice(pair * 2 * HD, (pair + 1) * 2 * HD)
            queries = paired(stripes_ref, 0, pair, slot, heads)
            grads = paired(stripes_ref, 1, pair, slot, heads)
            scores = dot(queries, enc_ref[0, slot, :, cols], 1, 1) * SCALE
            d_weights = dot(grads, enc_ref[1, slot, :, cols], 1, 1)
            weights = jnp.exp(scores - columns[:, pair : pair + 1]) * live
            d_scores = weights * (d_weights - columns[:, pairs + pair : pairs + pair + 1]) * SCALE
            weights_ref[slot * pairs + pair] = weights.astype(jnp.bfloat16)
            scores_ref[slot * pairs + pair] = d_scores.astype(jnp.bfloat16)
    for slot in range(slots):
        for pair in range(pairs):
            cols = slice(pair * 2 * HD, (pair + 1) * 2 * HD)
            for which, ref in enumerate((weights_ref, scores_ref)):
                right = enc_ref[1 - which, slot, :, cols]
                rows = dot(ref[slot * pairs + pair], right, 1, 0).astype(jnp.bfloat16)
                for side in range(2):
                    for half in range(2):
                        stripe = (which * heads + 2 * pair + side) * 2 + half
                        at = side * CH + half * HALF
                        out_ref[stripe, slot] = rows[at : at + HALF, side * HD : (side + 1) * HD]


def slot_side(
    meta_ref, stripes_ref, enc_ref, stats_ref, sink_ref, after_ref, *refs, me_at
):
    out_ref, weights_ref, scores_ref = refs
    heads = enc_ref.shape[3] // HD
    pairs = heads // 2
    count = out_ref.shape[1]
    first = pl.program_id(0) * count
    for step in range(count):
        slot = first + step
        log_total, deltas, live = slot_stats(meta_ref, stats_ref, sink_ref, slot, me_at)
        for pair in range(pairs):
            cols = slice(pair * 2 * HD, (pair + 1) * 2 * HD)
            queries = paired(stripes_ref, 0, pair, slot, heads)
            grads = paired(stripes_ref, 1, pair, slot, heads)
            scores = dot(enc_ref[0, slot, :, cols], queries, 1, 1) * SCALE
            d_weights = dot(enc_ref[1, slot, :, cols], grads, 1, 1)
            weights = jnp.exp(scores - log_total[pair : pair + 1]) * live
            d_scores = weights * (d_weights - deltas[pair : pair + 1]) * SCALE
            weights_ref[step * pairs + pair] = weights.astype(jnp.bfloat16)
            scores_ref[step * pairs + pair] = d_scores.astype(jnp.bfloat16)
    for step in range(count):
        slot = first + step
        for pair in range(pairs):
            cols = slice(pair * 2 * HD, (pair + 1) * 2 * HD)
            for which, ref in enumerate((scores_ref, weights_ref)):
                right = paired(stripes_ref, which, pair, slot, heads)
                rows = dot(ref[step * pairs + pair], right, 1, 0)
                out_ref[which, step, :, cols] = rows.astype(jnp.bfloat16)


def sink_side(meta_ref, stats_ref, sink_ref, after_ref, out_ref, *, pos_at, live_at, spans):
    sink = sink_ref[...]

    def body(span, total):
        here = pos_at + 2 * span - NB
        live = meta_ref[live_at + span].astype(jnp.float32)
        _, deltas, part = joined(stats_ref[meta_ref[here]], stats_ref[meta_ref[here + 1]], sink)
        return total - part * deltas * live

    out_ref[...] = lax.fori_loop(1, spans, body, jnp.zeros_like(sink), unroll=7)


def routing(owner_row, doc_row, seq_index, slots, seq_count):
    neigh_count, spans = owner_row.shape[0], doc_row.shape[0]
    neigh_ids = jnp.arange(neigh_count, dtype=jnp.int32)
    before = neigh_ids[None, :] < neigh_ids[:, None]
    same_owner = owner_row[None, :] == owner_row[:, None]
    slot_of = jnp.sum(before & same_owner, axis=1).astype(jnp.int32)
    place = owner_row * slots + slot_of
    other = jnp.flip(place.reshape(spans, NB), axis=1).reshape(-1)
    span_ids = jnp.arange(spans, dtype=jnp.int32)
    live = ((span_ids >= 1) & (doc_row == 0)).astype(jnp.int32)
    next_live = jnp.concatenate([live[1:], jnp.zeros((1,), jnp.int32)])
    reader = jnp.minimum(neigh_ids // NB + 1, spans - 1)
    code = reader + 64 * jnp.repeat(next_live, NB) + 128 * other
    flat = jnp.arange(slots * seq_count, dtype=jnp.int32)
    codes = jnp.sum(jnp.where(place[None, :] == flat[:, None], code[None, :], 0), axis=1)
    first = (seq_index * slots).astype(jnp.int32).reshape(1)
    return jnp.concatenate([codes, place, live, first])


def on_device(queries, encodings, sink, owner, doc_start, d_out):
    seq_count = lax.axis_size("seq")
    seq_index = lax.axis_index("seq")
    tokens, width = queries.shape[1:]
    spans_here = tokens // CH
    heads = width // HD
    pairs = heads // 2
    slots = encodings.shape[2]
    spans, neighs = doc_start.shape[1], owner.shape[1]
    places = seq_count * slots
    pos_at = places
    live_at = pos_at + neighs
    me_at = live_at + spans
    bf16 = jnp.bfloat16
    f32 = jnp.float32
    stripe = (HALF, HD)
    flops = 4 * NL * CH * width * slots

    def everywhere(block):
        return lax.all_to_all(block, "seq", split_axis=0, concat_axis=0, tiled=True)

    def call(kernel, name, out, *operands, in_specs=None, out_specs=IN_VMEM, work=0, limit=16, **kw):
        if in_specs is None:
            in_specs = [IN_SMEM if x.dtype == jnp.int32 else IN_VMEM for x in operands]
        return pl.pallas_call(
            kernel,
            in_specs=in_specs,
            out_specs=out_specs,
            out_shape=out,
            compiler_params=pltpu.CompilerParams(vmem_limit_bytes=limit * MIB),
            cost_estimate=pl.CostEstimate(
                flops=work, bytes_accessed=sum(x.nbytes for x in operands), transcendentals=0
            ),
            name=name,
            **kw,
        )(*(in_hbm(x) if spec is IN_HBM else x for x, spec in zip(operands, in_specs)))

    meta = routing(owner[0], doc_start[0], seq_index, slots, seq_count)
    sink_rows = jnp.repeat(sink.reshape(pairs, 2), CH, axis=1)
    enc = encodings[0]

    def struct(shape, dtype=bf16):
        return jax.ShapeDtypeStruct(shape, dtype)

    def in_hbm(x):
        return pltpu.with_memory_space_constraint(x, pltpu.HBM)

    def by_slots(shape, axis):
        block = tuple(n // STEPS if d == axis else n for d, n in enumerate(shape))
        return pl.BlockSpec(block, lambda i: tuple(i if d == axis else 0 for d in range(len(shape))))

    cut_shape = (2, heads, 2, spans_here) + stripe
    cut = call(
        cut_stripes,
        "cut",
        pltpu.HBM(cut_shape, bf16),
        queries[0],
        d_out[0],
        in_specs=[IN_HBM, IN_HBM],
        out_specs=IN_HBM,
        scratch_shapes=[
            pltpu.VMEM((2, tokens, width), bf16),
            pltpu.VMEM(cut_shape, bf16),
            pltpu.SemaphoreType.DMA((2,)),
            pltpu.SemaphoreType.DMA((2,)),
        ],
    )
    all_spans = everywhere(cut.reshape((seq_count, spans_here) + stripe))
    spread = call(
        spread_spans,
        "spread",
        struct((places,) + stripe),
        meta,
        all_spans.reshape((spans,) + stripe),
        sink_rows,
    )
    stripes = everywhere(spread.reshape((seq_count, slots) + stripe))

    stats_shape = (seq_count, slots, heads, HD)
    stats = call(
        stats_of,
        "stats",
        struct(stats_shape, f32),
        stripes,
        enc,
        grid=(STEPS,),
        out_specs=by_slots(stats_shape, 1),
        work=flops,
    )
    all_stats = everywhere(stats).reshape(places, heads, HD)
    whole = (meta, stripes, enc, all_stats, sink_rows)
    partials = call(
        functools.partial(token_side, me_at=me_at),
        "token_side",
        struct(stripes.shape),
        *whole,
        work=2 * flops,
        scratch_shapes=[pltpu.VMEM((slots * pairs, NL, NL), bf16)] * 2,
    )
    returned = everywhere(partials).reshape((places,) + stripe)
    summed = call(
        functools.partial(add_partials, pos_at=pos_at),
        "add_partials",
        pltpu.HBM((spans,) + stripe, bf16),
        meta,
        returned,
    )
    final = everywhere(summed.reshape((seq_count, spans_here) + stripe))
    enc_grads = call(
        functools.partial(slot_side, me_at=me_at),
        "slot_side",
        struct(enc.shape),
        *whole,
        summed,
        in_specs=[IN_SMEM] + [IN_VMEM] * 4 + [IN_HBM],
        grid=(STEPS,),
        out_specs=by_slots(enc.shape, 1),
        work=2 * flops,
        scratch_shapes=[pltpu.VMEM((slots // STEPS * pairs, NL, NL), bf16)] * 2,
    )
    sink_lanes = call(
        functools.partial(sink_side, pos_at=pos_at, live_at=live_at, spans=spans),
        "sink_side",
        struct((pairs, HD), f32),
        meta,
        all_stats,
        sink_rows,
        summed,
        in_specs=[IN_SMEM, IN_VMEM, IN_VMEM, IN_HBM],
        work=spans * 4096,
    )
    sink_part = jnp.sum(sink_lanes.reshape(heads, CH), axis=1)
    sink_total = sink_part + lax.ppermute(sink_part, "dp", [(0, 1), (1, 0)])

    rows = pl.BlockSpec((tokens, width), lambda: (0, 0))
    attended, grad_query = call(
        join_stripes, "join", [struct((tokens, width))] * 2, final, out_specs=[rows, rows]
    )
    return attended[None], grad_query[None], enc_grads[None], sink_total


def solution(mesh):
    in_specs = (
        P("dp", "seq", "mp"),
        P("dp", None, "seq", None, "mp"),
        P("mp"),
        P("dp", None),
        P("dp", None),
        P("dp", "seq", "mp"),
    )
    out_specs = (
        P("dp", "seq", "mp"),
        P("dp", "seq", "mp"),
        P("dp", None, "seq", None, "mp"),
        P("mp"),
    )
    return jax.shard_map(
        on_device, mesh=mesh, in_specs=in_specs, out_specs=out_specs, check_vma=False
    )
```

```python
import functools

import jax
import jax.numpy as jnp
from jax import lax
from jax.experimental import pallas as pl
from jax.experimental.pallas import tpu as pltpu
from jax.sharding import PartitionSpec as P

HD = 128
CH = 64
NB = 2
NL = 128
HALF = CH // 2
SCALE = HD ** (-0.5)
MIB = 1024 * 1024
STEPS = 2
GROUPS = 16
PLACES, LIVE = GROUPS, GROUPS + 1
IN_VMEM = pl.BlockSpec(memory_space=pltpu.VMEM)
IN_HBM = pl.BlockSpec(memory_space=pltpu.HBM)
IN_SMEM = pl.BlockSpec(memory_space=pltpu.SMEM)


def cut_stripes(query_hbm, grad_hbm, turn_ref, out_hbm, done_ref, *scratch):
    rows_ref, out_ref, in_sems, out_sems = scratch
    done_ref[...] = jnp.zeros_like(done_ref)
    whiches, heads, halves, spans = out_ref.shape[:4]
    loads, stores = [], []
    for which, ref in enumerate((query_hbm, grad_hbm)):
        loads.append(pltpu.make_async_copy(ref, rows_ref.at[which], in_sems.at[which]))
        stores.append(
            pltpu.make_async_copy(out_ref.at[which], out_hbm.at[which], out_sems.at[which])
        )
        loads[which].start()
    for which in range(whiches):
        loads[which].wait()
        for head in range(heads):
            for half in range(halves):
                for span in range(spans):
                    row = span * CH + half * HALF
                    out_ref[which, head, half, span] = rows_ref[
                        which, row : row + HALF, head * HD : (head + 1) * HD
                    ]
        stores[which].start()
    for store in stores:
        store.wait()


def join_stripes(in_ref, attended_ref, query_ref):
    spans, heads = in_ref.shape[1], attended_ref.shape[1] // HD
    for which, ref in enumerate((attended_ref, query_ref)):
        for head in range(heads):
            for half in range(2):
                stripe = (which * heads + head) * 2 + half
                for span in range(spans):
                    row = span * CH + half * HALF
                    ref[row : row + HALF, head * HD : (head + 1) * HD] = in_ref[stripe, span]


def spread_spans(meta_ref, in_ref, sink_ref, out_ref):
    def body(group, carry):
        for slot in range(GROUPS):
            out_ref[group, slot] = in_ref[meta_ref[group, slot] & 63]
        return carry

    lax.fori_loop(0, out_ref.shape[0], body, 0)


def add_partials(meta_ref, in_ref, out_ref):
    def body(span, carry):
        here = 2 * span - NB
        left = in_ref[meta_ref[PLACES, here]].astype(jnp.float32)
        right = in_ref[meta_ref[PLACES, here + 1]].astype(jnp.float32)
        out_ref[span] = (left + right).astype(jnp.bfloat16)
        return carry

    out_ref[0] = jnp.zeros(out_ref.shape[1:], jnp.bfloat16)
    lax.fori_loop(1, out_ref.shape[0], body, 0, unroll=9)


def paired(stripes_ref, which, pair, slot, heads):
    nothing = jnp.zeros((CH, HD), jnp.bfloat16)
    blocks = []
    for head in (2 * pair, 2 * pair + 1):
        at = (which * heads + head) * 2
        blocks.append(jnp.concatenate([stripes_ref[at, slot], stripes_ref[at + 1, slot]], axis=0))
    return jnp.concatenate(
        [
            jnp.concatenate([blocks[0], nothing], axis=1),
            jnp.concatenate([nothing, blocks[1]], axis=1),
        ],
        axis=0,
    )


def dot(left, right, left_dim, right_dim):
    return lax.dot_general(
        left, right, (((left_dim,), (right_dim,)), ((), ())), preferred_element_type=jnp.float32
    )


def stats_of(stripes_ref, enc_ref, out_ref):
    heads = enc_ref.shape[3] // HD
    pairs = heads // 2
    count = out_ref.shape[1]
    first = pl.program_id(0) * count
    for step in range(count):
        slot = first + step
        for pair in range(pairs):
            cols = slice(pair * 2 * HD, (pair + 1) * 2 * HD)
            queries = paired(stripes_ref, 0, pair, slot, heads)
            grads = paired(stripes_ref, 1, pair, slot, heads)
            scores = dot(enc_ref[0, slot, :, cols], queries, 1, 1) * SCALE
            d_weights = dot(enc_ref[1, slot, :, cols], grads, 1, 1)
            top = jnp.max(scores, axis=0, keepdims=True)
            powers = jnp.exp(scores - top)
            total = jnp.sum(powers, axis=0, keepdims=True)
            out_ref[0, step, pair : pair + 1] = top + jnp.log(total)
            delta = jnp.sum(powers * d_weights, axis=0, keepdims=True) / total
            out_ref[0, step, pairs + pair : pairs + pair + 1] = delta
    for dest in range(1, out_ref.shape[0]):
        out_ref[dest] = out_ref[0]


def joined(mine, other, sink):
    pairs = sink.shape[0]
    log_a, log_b = mine[:pairs], other[:pairs]
    top = jnp.maximum(jnp.maximum(log_a, log_b), sink)
    part_a, part_b, part_s = jnp.exp(log_a - top), jnp.exp(log_b - top), jnp.exp(sink - top)
    total = part_a + part_b + part_s
    deltas = (part_a * mine[pairs:] + part_b * other[pairs:]) / total
    return top + jnp.log(total), deltas, part_s / total


def slot_stats(meta_ref, stats_ref, sink_ref, slot):
    group = lax.axis_index("seq")
    mine_at = group * GROUPS + slot
    code = meta_ref[group, slot]
    live = ((code >> 6) & 1).astype(jnp.float32)
    log_total, deltas, _ = joined(stats_ref[mine_at], stats_ref[code >> 7], sink_ref[...])
    return log_total, deltas, live


def token_side(
    meta_ref, stripes_ref, enc_ref, stats_ref, sink_ref, out_ref, weights_ref, scores_ref
):
    heads = enc_ref.shape[3] // HD
    pairs = heads // 2
    slots = enc_ref.shape[1]
    for slot in range(slots):
        log_total, deltas, live = slot_stats(meta_ref, stats_ref, sink_ref, slot)
        spare = jnp.zeros((8 - 2 * pairs, 2 * CH), jnp.float32)
        columns = jnp.concatenate([log_total, deltas, spare], axis=0).T
        for pair in range(pairs):
            cols = slice(pair * 2 * HD, (pair + 1) * 2 * HD)
            queries = paired(stripes_ref, 0, pair, slot, heads)
            grads = paired(stripes_ref, 1, pair, slot, heads)
            scores = dot(queries, enc_ref[0, slot, :, cols], 1, 1) * SCALE
            d_weights = dot(grads, enc_ref[1, slot, :, cols], 1, 1)
            weights = jnp.exp(scores - columns[:, pair : pair + 1]) * live
            d_scores = weights * (d_weights - columns[:, pairs + pair : pairs + pair + 1]) * SCALE
            weights_ref[slot * pairs + pair] = weights.astype(jnp.bfloat16)
            scores_ref[slot * pairs + pair] = d_scores.astype(jnp.bfloat16)
    for slot in range(slots):
        for pair in range(pairs):
            cols = slice(pair * 2 * HD, (pair + 1) * 2 * HD)
            for which, ref in enumerate((weights_ref, scores_ref)):
                right = enc_ref[1 - which, slot, :, cols]
                rows = dot(ref[slot * pairs + pair], right, 1, 0).astype(jnp.bfloat16)
                for side in range(2):
                    for half in range(2):
                        stripe = (which * heads + 2 * pair + side) * 2 + half
                        at = side * CH + half * HALF
                        out_ref[stripe, slot] = rows[at : at + HALF, side * HD : (side + 1) * HD]


def slot_side(
    meta_ref, stripes_ref, enc_ref, stats_ref, sink_ref, after_ref, *refs
):
    out_ref, weights_ref, scores_ref = refs
    heads = enc_ref.shape[3] // HD
    pairs = heads // 2
    count = out_ref.shape[1]
    first = pl.program_id(0) * count
    for step in range(count):
        slot = first + step
        log_total, deltas, live = slot_stats(meta_ref, stats_ref, sink_ref, slot)
        for pair in range(pairs):
            cols = slice(pair * 2 * HD, (pair + 1) * 2 * HD)
            queries = paired(stripes_ref, 0, pair, slot, heads)
            grads = paired(stripes_ref, 1, pair, slot, heads)
            scores = dot(enc_ref[0, slot, :, cols], queries, 1, 1) * SCALE
            d_weights = dot(enc_ref[1, slot, :, cols], grads, 1, 1)
            weights = jnp.exp(scores - log_total[pair : pair + 1]) * live
            d_scores = weights * (d_weights - deltas[pair : pair + 1]) * SCALE
            weights_ref[step * pairs + pair] = weights.astype(jnp.bfloat16)
            scores_ref[step * pairs + pair] = d_scores.astype(jnp.bfloat16)
    for step in range(count):
        slot = first + step
        for pair in range(pairs):
            cols = slice(pair * 2 * HD, (pair + 1) * 2 * HD)
            for which, ref in enumerate((scores_ref, weights_ref)):
                right = paired(stripes_ref, which, pair, slot, heads)
                rows = dot(ref[step * pairs + pair], right, 1, 0)
                out_ref[which, step, :, cols] = rows.astype(jnp.bfloat16)


def sink_side(meta_ref, stats_ref, sink_ref, after_ref, out_ref, *, spans):
    sink = sink_ref[...]

    def body(span, total):
        here = 2 * span - NB
        live = meta_ref[LIVE, span].astype(jnp.float32)
        left, right = stats_ref[meta_ref[PLACES, here]], stats_ref[meta_ref[PLACES, here + 1]]
        _, deltas, part = joined(left, right, sink)
        return total - part * deltas * live

    out_ref[...] = lax.fori_loop(1, spans, body, jnp.zeros_like(sink), unroll=7)


def route(owner_ref, doc_ref, sink_ref, after_ref, meta_ref, rows_ref):
    f32, i32 = jnp.float32, jnp.int32
    groups, neighs, spans = GROUPS, owner_ref.shape[1], doc_ref.shape[1]

    def ids(shape, dim):
        return lax.broadcasted_iota(i32, shape, dim)

    def one_hot(hits):
        return hits.astype(f32).astype(jnp.bfloat16)

    owner = owner_ref[...]
    in_group = one_hot(ids((groups, neighs), 0) == owner)
    earlier = one_hot(ids((neighs, neighs), 0) < ids((neighs, neighs), 1))
    rank = dot(in_group, earlier, 1, 0) * in_group.astype(f32)
    slot = jnp.sum(rank, axis=0, keepdims=True).astype(i32)
    place = owner * groups + slot
    lane = ids((1, neighs), 1)
    other = jnp.where(lane % 2 == 0, pltpu.roll(place, neighs - 1, 1), pltpu.roll(place, 1, 1))
    reader = lane // NB + 1
    span = ids((1, spans), 1)
    live = ((span >= 1) & (doc_ref[...] == 0)).astype(f32)
    reads = one_hot(ids((spans, neighs), 0) == ids((spans, neighs), 1) // NB + 1)
    read_live = dot(live.astype(jnp.bfloat16), reads, 1, 0)
    low = jnp.minimum(reader, spans - 1).astype(f32) + 64.0 * read_live
    in_slot = one_hot(ids((groups, neighs), 0) == slot)

    def by_slot(row):
        return dot(in_group * row.astype(jnp.bfloat16), in_slot, 1, 1).astype(i32)

    codes = by_slot(low) + 128 * by_slot(other.astype(f32))
    meta_ref[...] = jnp.zeros_like(meta_ref)
    meta_ref[0:groups, 0:groups] = codes
    meta_ref[groups : groups + 1] = place
    meta_ref[groups + 1 : groups + 2, 0:spans] = live.astype(i32)
    left = ids((1, 2 * CH), 1) < CH
    for pair in range(rows_ref.shape[0]):
        rows_ref[pair : pair + 1] = jnp.where(left, sink_ref[2 * pair], sink_ref[2 * pair + 1])


def on_device(queries, encodings, sink, owner, doc_start, d_out):
    seq_count = lax.axis_size("seq")
    tokens, width = queries.shape[1:]
    spans_here = tokens // CH
    heads = width // HD
    pairs = heads // 2
    slots = encodings.shape[2]
    spans = doc_start.shape[1]
    places = seq_count * slots
    bf16 = jnp.bfloat16
    f32 = jnp.float32
    stripe = (HALF, HD)
    flops = 4 * NL * CH * width * slots

    def everywhere(block):
        return lax.all_to_all(block, "seq", split_axis=0, concat_axis=0, tiled=True)

    def call(kernel, name, out, *operands, in_specs=None, out_specs=IN_VMEM, work=0, limit=16, **kw):
        if in_specs is None:
            in_specs = [IN_SMEM if x.dtype == jnp.int32 else IN_VMEM for x in operands]
        return pl.pallas_call(
            kernel,
            in_specs=in_specs,
            out_specs=out_specs,
            out_shape=out,
            compiler_params=pltpu.CompilerParams(vmem_limit_bytes=limit * MIB),
            cost_estimate=pl.CostEstimate(
                flops=work, bytes_accessed=sum(x.nbytes for x in operands), transcendentals=0
            ),
            name=name,
            **kw,
        )(*(in_hbm(x) if spec is IN_HBM else x for x, spec in zip(operands, in_specs)))

    enc = encodings[0]

    def struct(shape, dtype=bf16):
        return jax.ShapeDtypeStruct(shape, dtype)

    def in_hbm(x):
        return pltpu.with_memory_space_constraint(x, pltpu.HBM)

    def by_slots(shape, axis):
        block = tuple(n // STEPS if d == axis else n for d, n in enumerate(shape))
        return pl.BlockSpec(block, lambda i: tuple(i if d == axis else 0 for d in range(len(shape))))

    pairs_of_first = [(2 * i, 2 * (i ^ 1)) for i in range(seq_count)]
    turn = lax.ppermute(sink, ("seq", "dp"), pairs_of_first)
    cut_shape = (2, heads, 2, spans_here) + stripe
    cut, done = call(
        cut_stripes,
        "cut",
        [pltpu.HBM(cut_shape, bf16), struct((8, HD), f32)],
        queries[0],
        d_out[0],
        turn,
        in_specs=[IN_HBM, IN_HBM, IN_VMEM],
        out_specs=[IN_HBM, IN_VMEM],
        scratch_shapes=[
            pltpu.VMEM((2, tokens, width), bf16),
            pltpu.VMEM(cut_shape, bf16),
            pltpu.SemaphoreType.DMA((2,)),
            pltpu.SemaphoreType.DMA((2,)),
        ],
    )
    meta, sink_rows = call(
        route,
        "route",
        [struct((24, HD), jnp.int32), struct((pairs, HD), f32)],
        owner,
        doc_start,
        sink,
        done,
        in_specs=[IN_VMEM, IN_VMEM, IN_SMEM, IN_VMEM],
        out_specs=[IN_VMEM, IN_VMEM],
    )
    all_spans = everywhere(cut.reshape((seq_count, spans_here) + stripe))
    spread = call(
        spread_spans,
        "spread",
        struct((seq_count, slots) + stripe),
        meta,
        all_spans.reshape((spans,) + stripe),
        sink_rows,
    )
    stripes = everywhere(spread)

    stats_shape = (seq_count, slots, heads, HD)
    stats = call(
        stats_of,
        "stats",
        struct(stats_shape, f32),
        stripes,
        enc,
        grid=(STEPS,),
        out_specs=by_slots(stats_shape, 1),
        work=flops,
    )
    all_stats = everywhere(stats).reshape(places, heads, HD)
    whole = (meta, stripes, enc, all_stats, sink_rows)
    partials = call(
        token_side,
        "token_side",
        struct(stripes.shape),
        *whole,
        work=2 * flops,
        scratch_shapes=[pltpu.VMEM((slots * pairs, NL, NL), bf16)] * 2,
    )
    returned = everywhere(partials).reshape((places,) + stripe)
    summed = call(
        add_partials,
        "add_partials",
        pltpu.HBM((spans,) + stripe, bf16),
        meta,
        returned,
    )
    final = everywhere(summed.reshape((seq_count, spans_here) + stripe))
    enc_grads = call(
        slot_side,
        "slot_side",
        struct(enc.shape),
        *whole,
        summed,
        in_specs=[IN_SMEM] + [IN_VMEM] * 4 + [IN_HBM],
        grid=(STEPS,),
        out_specs=by_slots(enc.shape, 1),
        work=2 * flops,
        scratch_shapes=[pltpu.VMEM((slots // STEPS * pairs, NL, NL), bf16)] * 2,
    )
    sink_lanes = call(
        functools.partial(sink_side, spans=spans),
        "sink_side",
        struct((pairs, HD), f32),
        meta,
        all_stats,
        sink_rows,
        summed,
        in_specs=[IN_SMEM, IN_VMEM, IN_VMEM, IN_HBM],
        work=spans * 4096,
    )
    sink_part = jnp.sum(sink_lanes.reshape(heads, CH), axis=1)
    sink_total = sink_part + lax.ppermute(sink_part, "dp", [(0, 1), (1, 0)])

    rows = pl.BlockSpec((tokens, width), lambda: (0, 0))
    attended, grad_query = call(
        join_stripes, "join", [struct((tokens, width))] * 2, final, out_specs=[rows, rows]
    )
    return attended[None], grad_query[None], enc_grads[None], sink_total


def solution(mesh):
    in_specs = (
        P("dp", "seq", "mp"),
        P("dp", None, "seq", None, "mp"),
        P("mp"),
        P("dp", None),
        P("dp", None),
        P("dp", "seq", "mp"),
    )
    out_specs = (
        P("dp", "seq", "mp"),
        P("dp", "seq", "mp"),
        P("dp", None, "seq", None, "mp"),
        P("mp"),
    )
    return jax.shard_map(
        on_device, mesh=mesh, in_specs=in_specs, out_specs=out_specs, check_vma=False
    )
```

```python
import functools

import jax
import jax.numpy as jnp
from jax import lax
from jax.experimental import pallas as pl
from jax.experimental.pallas import tpu as pltpu
from jax.sharding import PartitionSpec as P

HD = 128
CH = 64
NB = 2
NL = 128
HALF = CH // 2
SCALE = HD ** (-0.5)
MIB = 1024 * 1024
STEPS = 2
GROUPS = 16
PLACES, LIVE = GROUPS, GROUPS + 1
IN_VMEM = pl.BlockSpec(memory_space=pltpu.VMEM)
IN_HBM = pl.BlockSpec(memory_space=pltpu.HBM)
IN_SMEM = pl.BlockSpec(memory_space=pltpu.SMEM)


def cut_stripes(query_hbm, grad_hbm, turn_ref, out_hbm, done_ref, *scratch):
    rows_ref, out_ref, in_sems, out_sems = scratch
    done_ref[...] = jnp.zeros_like(done_ref)
    whiches, heads, halves, spans = out_ref.shape[:4]
    loads, stores = [], []
    for which, ref in enumerate((query_hbm, grad_hbm)):
        loads.append(pltpu.make_async_copy(ref, rows_ref.at[which], in_sems.at[which]))
        stores.append(
            pltpu.make_async_copy(out_ref.at[which], out_hbm.at[which], out_sems.at[which])
        )
        loads[which].start()
    for which in range(whiches):
        loads[which].wait()
        for head in range(heads):
            for half in range(halves):
                for span in range(spans):
                    row = span * CH + half * HALF
                    out_ref[which, head, half, span] = rows_ref[
                        which, row : row + HALF, head * HD : (head + 1) * HD
                    ]
        stores[which].start()
    for store in stores:
        store.wait()


def join_stripes(in_ref, attended_ref, query_ref):
    spans, heads = in_ref.shape[1], attended_ref.shape[1] // HD
    for which, ref in enumerate((attended_ref, query_ref)):
        for head in range(heads):
            for half in range(2):
                stripe = (which * heads + head) * 2 + half
                for span in range(spans):
                    row = span * CH + half * HALF
                    ref[row : row + HALF, head * HD : (head + 1) * HD] = in_ref[stripe, span]


def spread_spans(meta_ref, in_ref, sink_ref, out_ref):
    for group in range(GROUPS):
        for slot in range(GROUPS):
            out_ref[group, slot] = in_ref[meta_ref[group, slot] & 63]


def add_partials(meta_ref, in_ref, out_ref):
    out_ref[0] = jnp.zeros(out_ref.shape[1:], jnp.bfloat16)
    for span in range(1, out_ref.shape[0]):
        left = in_ref[meta_ref[PLACES, NB * span - 2]].astype(jnp.float32)
        right = in_ref[meta_ref[PLACES, NB * span - 1]].astype(jnp.float32)
        out_ref[span] = (left + right).astype(jnp.bfloat16)


def paired(stripes_ref, which, pair, slot, heads):
    nothing = jnp.zeros((CH, HD), jnp.bfloat16)
    blocks = []
    for head in (2 * pair, 2 * pair + 1):
        at = (which * heads + head) * 2
        blocks.append(jnp.concatenate([stripes_ref[at, slot], stripes_ref[at + 1, slot]], axis=0))
    return jnp.concatenate(
        [
            jnp.concatenate([blocks[0], nothing], axis=1),
            jnp.concatenate([nothing, blocks[1]], axis=1),
        ],
        axis=0,
    )


def dot(left, right, left_dim, right_dim):
    return lax.dot_general(
        left, right, (((left_dim,), (right_dim,)), ((), ())), preferred_element_type=jnp.float32
    )


def stats_of(stripes_ref, enc_ref, out_ref):
    heads = enc_ref.shape[3] // HD
    pairs = heads // 2
    count = out_ref.shape[1]
    first = pl.program_id(0) * count
    for step in range(count):
        slot = first + step
        for pair in range(pairs):
            cols = slice(pair * 2 * HD, (pair + 1) * 2 * HD)
            queries = paired(stripes_ref, 0, pair, slot, heads)
            grads = paired(stripes_ref, 1, pair, slot, heads)
            scores = dot(enc_ref[0, slot, :, cols], queries, 1, 1) * SCALE
            d_weights = dot(enc_ref[1, slot, :, cols], grads, 1, 1)
            top = jnp.max(scores, axis=0, keepdims=True)
            powers = jnp.exp(scores - top)
            total = jnp.sum(powers, axis=0, keepdims=True)
            out_ref[0, step, pair : pair + 1] = top + jnp.log(total)
            delta = jnp.sum(powers * d_weights, axis=0, keepdims=True) / total
            out_ref[0, step, pairs + pair : pairs + pair + 1] = delta
    for dest in range(1, out_ref.shape[0]):
        out_ref[dest] = out_ref[0]


def joined(mine, other, sink):
    pairs = sink.shape[0]
    log_a, log_b = mine[:pairs], other[:pairs]
    top = jnp.maximum(jnp.maximum(log_a, log_b), sink)
    part_a, part_b, part_s = jnp.exp(log_a - top), jnp.exp(log_b - top), jnp.exp(sink - top)
    total = part_a + part_b + part_s
    deltas = (part_a * mine[pairs:] + part_b * other[pairs:]) / total
    return top + jnp.log(total), deltas, part_s / total


def slot_stats(meta_ref, stats_ref, sink_ref, slot):
    group = lax.axis_index("seq")
    mine_at = group * GROUPS + slot
    code = meta_ref[group, slot]
    live = ((code >> 6) & 1).astype(jnp.float32)
    log_total, deltas, _ = joined(stats_ref[mine_at], stats_ref[code >> 7], sink_ref[...])
    return log_total, deltas, live


def token_side(
    meta_ref, stripes_ref, enc_ref, stats_ref, sink_ref, out_ref, weights_ref, scores_ref
):
    heads = enc_ref.shape[3] // HD
    pairs = heads // 2
    slots = enc_ref.shape[1]
    for slot in range(slots):
        log_total, deltas, live = slot_stats(meta_ref, stats_ref, sink_ref, slot)
        spare = jnp.zeros((8 - 2 * pairs, 2 * CH), jnp.float32)
        columns = jnp.concatenate([log_total, deltas, spare], axis=0).T
        for pair in range(pairs):
            cols = slice(pair * 2 * HD, (pair + 1) * 2 * HD)
            queries = paired(stripes_ref, 0, pair, slot, heads)
            grads = paired(stripes_ref, 1, pair, slot, heads)
            scores = dot(queries, enc_ref[0, slot, :, cols], 1, 1) * SCALE
            d_weights = dot(grads, enc_ref[1, slot, :, cols], 1, 1)
            weights = jnp.exp(scores - columns[:, pair : pair + 1]) * live
            d_scores = weights * (d_weights - columns[:, pairs + pair : pairs + pair + 1]) * SCALE
            weights_ref[slot * pairs + pair] = weights.astype(jnp.bfloat16)
            scores_ref[slot * pairs + pair] = d_scores.astype(jnp.bfloat16)
    for slot in range(slots):
        for pair in range(pairs):
            cols = slice(pair * 2 * HD, (pair + 1) * 2 * HD)
            for which, ref in enumerate((weights_ref, scores_ref)):
                right = enc_ref[1 - which, slot, :, cols]
                rows = dot(ref[slot * pairs + pair], right, 1, 0).astype(jnp.bfloat16)
                for side in range(2):
                    for half in range(2):
                        stripe = (which * heads + 2 * pair + side) * 2 + half
                        at = side * CH + half * HALF
                        out_ref[stripe, slot] = rows[at : at + HALF, side * HD : (side + 1) * HD]


def slot_side(
    meta_ref, stripes_ref, enc_ref, stats_ref, sink_ref, after_ref, *refs
):
    out_ref, weights_ref, scores_ref = refs
    heads = enc_ref.shape[3] // HD
    pairs = heads // 2
    count = out_ref.shape[1]
    first = pl.program_id(0) * count
    for step in range(count):
        slot = first + step
        log_total, deltas, live = slot_stats(meta_ref, stats_ref, sink_ref, slot)
        for pair in range(pairs):
            cols = slice(pair * 2 * HD, (pair + 1) * 2 * HD)
            queries = paired(stripes_ref, 0, pair, slot, heads)
            grads = paired(stripes_ref, 1, pair, slot, heads)
            scores = dot(enc_ref[0, slot, :, cols], queries, 1, 1) * SCALE
            d_weights = dot(enc_ref[1, slot, :, cols], grads, 1, 1)
            weights = jnp.exp(scores - log_total[pair : pair + 1]) * live
            d_scores = weights * (d_weights - deltas[pair : pair + 1]) * SCALE
            weights_ref[step * pairs + pair] = weights.astype(jnp.bfloat16)
            scores_ref[step * pairs + pair] = d_scores.astype(jnp.bfloat16)
    for step in range(count):
        slot = first + step
        for pair in range(pairs):
            cols = slice(pair * 2 * HD, (pair + 1) * 2 * HD)
            for which, ref in enumerate((scores_ref, weights_ref)):
                right = paired(stripes_ref, which, pair, slot, heads)
                rows = dot(ref[step * pairs + pair], right, 1, 0)
                out_ref[which, step, :, cols] = rows.astype(jnp.bfloat16)


def sink_side(meta_ref, stats_ref, sink_ref, after_ref, out_ref, *, spans):
    sink = sink_ref[...]

    def body(span, total):
        here = 2 * span - NB
        live = meta_ref[LIVE, span].astype(jnp.float32)
        left, right = stats_ref[meta_ref[PLACES, here]], stats_ref[meta_ref[PLACES, here + 1]]
        _, deltas, part = joined(left, right, sink)
        return total - part * deltas * live

    out_ref[...] = lax.fori_loop(1, spans, body, jnp.zeros_like(sink), unroll=7)


def route(owner_ref, doc_ref, sink_ref, after_ref, meta_ref, rows_ref):
    f32, i32 = jnp.float32, jnp.int32
    groups, neighs, spans = GROUPS, owner_ref.shape[1], doc_ref.shape[1]

    def ids(shape, dim):
        return lax.broadcasted_iota(i32, shape, dim)

    def one_hot(hits):
        return hits.astype(f32).astype(jnp.bfloat16)

    owner = owner_ref[...]
    in_group = one_hot(ids((groups, neighs), 0) == owner)
    earlier = one_hot(ids((neighs, neighs), 0) < ids((neighs, neighs), 1))
    rank = dot(in_group, earlier, 1, 0) * in_group.astype(f32)
    slot = jnp.sum(rank, axis=0, keepdims=True).astype(i32)
    place = owner * groups + slot
    lane = ids((1, neighs), 1)
    other = jnp.where(lane % 2 == 0, pltpu.roll(place, neighs - 1, 1), pltpu.roll(place, 1, 1))
    reader = lane // NB + 1
    span = ids((1, spans), 1)
    live = ((span >= 1) & (doc_ref[...] == 0)).astype(f32)
    reads = one_hot(ids((spans, neighs), 0) == ids((spans, neighs), 1) // NB + 1)
    read_live = dot(live.astype(jnp.bfloat16), reads, 1, 0)
    low = jnp.minimum(reader, spans - 1).astype(f32) + 64.0 * read_live
    in_slot = one_hot(ids((groups, neighs), 0) == slot)

    def by_slot(row):
        return dot(in_group * row.astype(jnp.bfloat16), in_slot, 1, 1).astype(i32)

    codes = by_slot(low) + 128 * by_slot(other.astype(f32))
    meta_ref[...] = jnp.zeros_like(meta_ref)
    meta_ref[0:groups, 0:groups] = codes
    meta_ref[groups : groups + 1] = place
    meta_ref[groups + 1 : groups + 2, 0:spans] = live.astype(i32)
    left = ids((1, 2 * CH), 1) < CH
    for pair in range(rows_ref.shape[0]):
        rows_ref[pair : pair + 1] = jnp.where(left, sink_ref[2 * pair], sink_ref[2 * pair + 1])


def on_device(queries, encodings, sink, owner, doc_start, d_out):
    seq_count = lax.axis_size("seq")
    tokens, width = queries.shape[1:]
    spans_here = tokens // CH
    heads = width // HD
    pairs = heads // 2
    slots = encodings.shape[2]
    spans = doc_start.shape[1]
    places = seq_count * slots
    bf16 = jnp.bfloat16
    f32 = jnp.float32
    stripe = (HALF, HD)
    flops = 4 * NL * CH * width * slots

    def everywhere(block):
        return lax.all_to_all(block, "seq", split_axis=0, concat_axis=0, tiled=True)

    def call(kernel, name, out, *operands, in_specs=None, out_specs=IN_VMEM, work=0, limit=16, **kw):
        if in_specs is None:
            in_specs = [IN_SMEM if x.dtype == jnp.int32 else IN_VMEM for x in operands]
        return pl.pallas_call(
            kernel,
            in_specs=in_specs,
            out_specs=out_specs,
            out_shape=out,
            compiler_params=pltpu.CompilerParams(vmem_limit_bytes=limit * MIB),
            cost_estimate=pl.CostEstimate(
                flops=work, bytes_accessed=sum(x.nbytes for x in operands), transcendentals=0
            ),
            name=name,
            **kw,
        )(*(in_hbm(x) if spec is IN_HBM else x for x, spec in zip(operands, in_specs)))

    enc = encodings[0]

    def struct(shape, dtype=bf16):
        return jax.ShapeDtypeStruct(shape, dtype)

    def in_hbm(x):
        return pltpu.with_memory_space_constraint(x, pltpu.HBM)

    def by_slots(shape, axis):
        block = tuple(n // STEPS if d == axis else n for d, n in enumerate(shape))
        return pl.BlockSpec(block, lambda i: tuple(i if d == axis else 0 for d in range(len(shape))))

    pairs_of_first = [(2 * i, 2 * (i ^ 2)) for i in range(seq_count)]
    turn = lax.ppermute(sink, ("seq", "dp"), pairs_of_first)
    cut_shape = (2, heads, 2, spans_here) + stripe
    cut, done = call(
        cut_stripes,
        "cut",
        [pltpu.HBM(cut_shape, bf16), struct((8, HD), f32)],
        queries[0],
        d_out[0],
        turn,
        in_specs=[IN_HBM, IN_HBM, IN_VMEM],
        out_specs=[IN_HBM, IN_VMEM],
        scratch_shapes=[
            pltpu.VMEM((2, tokens, width), bf16),
            pltpu.VMEM(cut_shape, bf16),
            pltpu.SemaphoreType.DMA((2,)),
            pltpu.SemaphoreType.DMA((2,)),
        ],
    )
    meta, sink_rows = call(
        route,
        "route",
        [struct((24, HD), jnp.int32), struct((pairs, HD), f32)],
        owner,
        doc_start,
        sink,
        done,
        in_specs=[IN_VMEM, IN_VMEM, IN_SMEM, IN_VMEM],
        out_specs=[IN_VMEM, IN_VMEM],
    )
    all_spans = everywhere(cut.reshape((seq_count, spans_here) + stripe))
    spread = call(
        spread_spans,
        "spread",
        struct((seq_count, slots) + stripe),
        meta,
        all_spans.reshape((spans,) + stripe),
        sink_rows,
    )
    stripes = everywhere(spread)

    stats_shape = (seq_count, slots, heads, HD)
    stats = call(
        stats_of,
        "stats",
        struct(stats_shape, f32),
        stripes,
        enc,
        grid=(STEPS,),
        out_specs=by_slots(stats_shape, 1),
        work=flops,
    )
    all_stats = everywhere(stats).reshape(places, heads, HD)
    whole = (meta, stripes, enc, all_stats, sink_rows)
    partials = call(
        token_side,
        "token_side",
        struct(stripes.shape),
        *whole,
        work=2 * flops,
        scratch_shapes=[pltpu.VMEM((slots * pairs, NL, NL), bf16)] * 2,
    )
    returned = everywhere(partials).reshape((places,) + stripe)
    summed = call(
        add_partials,
        "add_partials",
        pltpu.HBM((spans,) + stripe, bf16),
        meta,
        returned,
    )
    final = everywhere(summed.reshape((seq_count, spans_here) + stripe))
    enc_grads = call(
        slot_side,
        "slot_side",
        struct(enc.shape),
        *whole,
        summed,
        in_specs=[IN_SMEM] + [IN_VMEM] * 4 + [IN_HBM],
        grid=(STEPS,),
        out_specs=by_slots(enc.shape, 1),
        work=2 * flops,
        scratch_shapes=[pltpu.VMEM((slots // STEPS * pairs, NL, NL), bf16)] * 2,
    )
    sink_lanes = call(
        functools.partial(sink_side, spans=spans),
        "sink_side",
        struct((pairs, HD), f32),
        meta,
        all_stats,
        sink_rows,
        summed,
        in_specs=[IN_SMEM, IN_VMEM, IN_VMEM, IN_HBM],
        work=spans * 4096,
    )
    sink_part = jnp.sum(sink_lanes.reshape(heads, CH), axis=1)
    sink_total = sink_part + lax.ppermute(sink_part, "dp", [(0, 1), (1, 0)])

    rows = pl.BlockSpec((tokens, width), lambda: (0, 0))
    attended, grad_query = call(
        join_stripes, "join", [struct((tokens, width))] * 2, final, out_specs=[rows, rows]
    )
    return attended[None], grad_query[None], enc_grads[None], sink_total


def solution(mesh):
    in_specs = (
        P("dp", "seq", "mp"),
        P("dp", None, "seq", None, "mp"),
        P("mp"),
        P("dp", None),
        P("dp", None),
        P("dp", "seq", "mp"),
    )
    out_specs = (
        P("dp", "seq", "mp"),
        P("dp", "seq", "mp"),
        P("dp", None, "seq", None, "mp"),
        P("mp"),
    )
    return jax.shard_map(
        on_device, mesh=mesh, in_specs=in_specs, out_specs=out_specs, check_vma=False
    )
```

```python
import functools

import jax
import jax.numpy as jnp
from jax import lax
from jax.experimental import pallas as pl
from jax.experimental.pallas import tpu as pltpu
from jax.sharding import PartitionSpec as P

HD = 128
CH = 64
NB = 2
NL = 128
HALF = CH // 2
SCALE = HD ** (-0.5)
MIB = 1024 * 1024
STEPS = 2
GROUPS = 16
PLACES, LIVE = GROUPS, GROUPS + 1
IN_VMEM = pl.BlockSpec(memory_space=pltpu.VMEM)
IN_HBM = pl.BlockSpec(memory_space=pltpu.HBM)
IN_SMEM = pl.BlockSpec(memory_space=pltpu.SMEM)


def cut_stripes(query_hbm, grad_hbm, turn_ref, out_hbm, done_ref, *scratch):
    rows_ref, out_ref, in_sems, out_sems = scratch
    done_ref[...] = jnp.zeros_like(done_ref)
    _, heads, halves, spans = out_ref.shape[:4]
    steps = [(which, span) for which in range(2) for span in range(0, spans, 2)]
    loads, stores = [], []
    for step, (which, span) in enumerate(steps):
        rows = pl.ds(span * CH, 2 * CH)
        source = (query_hbm, grad_hbm)[which].at[rows]
        loads.append(pltpu.make_async_copy(source, rows_ref.at[which, rows], in_sems.at[step]))
        loads[step].start()
    for step, (which, first) in enumerate(steps):
        loads[step].wait()
        for head in range(heads):
            for half in range(halves):
                for span in (first, first + 1):
                    row = span * CH + half * HALF
                    out_ref[which, head, half, span] = rows_ref[
                        which, row : row + HALF, head * HD : (head + 1) * HD
                    ]
        at = (which, slice(None), slice(None), pl.ds(first, 2))
        stores.append(pltpu.make_async_copy(out_ref.at[at], out_hbm.at[at], out_sems.at[step]))
        stores[step].start()
    for store in stores:
        store.wait()


def join_stripes(in_ref, attended_ref, query_ref):
    spans, heads = in_ref.shape[1], attended_ref.shape[1] // HD
    for which, ref in enumerate((attended_ref, query_ref)):
        for head in range(heads):
            for half in range(2):
                stripe = (which * heads + head) * 2 + half
                for span in range(spans):
                    row = span * CH + half * HALF
                    ref[row : row + HALF, head * HD : (head + 1) * HD] = in_ref[stripe, span]


def spread_spans(meta_ref, in_ref, sink_ref, out_ref):
    for group in range(GROUPS):
        for slot in range(GROUPS):
            out_ref[group, slot] = in_ref[meta_ref[group, slot] & 63]


def add_partials(meta_ref, in_ref, out_ref):
    out_ref[0] = jnp.zeros(out_ref.shape[1:], jnp.bfloat16)
    for span in range(1, out_ref.shape[0]):
        left = in_ref[meta_ref[PLACES, NB * span - 2]].astype(jnp.float32)
        right = in_ref[meta_ref[PLACES, NB * span - 1]].astype(jnp.float32)
        out_ref[span] = (left + right).astype(jnp.bfloat16)


def paired(stripes_ref, which, pair, slot, heads):
    nothing = jnp.zeros((CH, HD), jnp.bfloat16)
    blocks = []
    for head in (2 * pair, 2 * pair + 1):
        at = (which * heads + head) * 2
        blocks.append(jnp.concatenate([stripes_ref[at, slot], stripes_ref[at + 1, slot]], axis=0))
    return jnp.concatenate(
        [
            jnp.concatenate([blocks[0], nothing], axis=1),
            jnp.concatenate([nothing, blocks[1]], axis=1),
        ],
        axis=0,
    )


def dot(left, right, left_dim, right_dim):
    return lax.dot_general(
        left, right, (((left_dim,), (right_dim,)), ((), ())), preferred_element_type=jnp.float32
    )


def stats_of(stripes_ref, enc_ref, out_ref):
    heads = enc_ref.shape[3] // HD
    pairs = heads // 2
    for slot in range(out_ref.shape[1]):
        for pair in range(pairs):
            cols = slice(pair * 2 * HD, (pair + 1) * 2 * HD)
            queries = paired(stripes_ref, 0, pair, slot, heads)
            grads = paired(stripes_ref, 1, pair, slot, heads)
            scores = dot(enc_ref[0, slot, :, cols], queries, 1, 1) * SCALE
            d_weights = dot(enc_ref[1, slot, :, cols], grads, 1, 1)
            top = jnp.max(scores, axis=0, keepdims=True)
            powers = jnp.exp(scores - top)
            total = jnp.sum(powers, axis=0, keepdims=True)
            out_ref[0, slot, pair : pair + 1] = top + jnp.log(total)
            delta = jnp.sum(powers * d_weights, axis=0, keepdims=True) / total
            out_ref[0, slot, pairs + pair : pairs + pair + 1] = delta
    for dest in range(1, out_ref.shape[0]):
        out_ref[dest] = out_ref[0]


def joined(mine, other, sink):
    pairs = sink.shape[0]
    log_a, log_b = mine[:pairs], other[:pairs]
    top = jnp.maximum(jnp.maximum(log_a, log_b), sink)
    part_a, part_b, part_s = jnp.exp(log_a - top), jnp.exp(log_b - top), jnp.exp(sink - top)
    total = part_a + part_b + part_s
    deltas = (part_a * mine[pairs:] + part_b * other[pairs:]) / total
    return top + jnp.log(total), deltas, part_s / total


def slot_stats(meta_ref, stats_ref, sink_ref, slot):
    group = lax.axis_index("seq")
    mine_at = group * GROUPS + slot
    code = meta_ref[group, slot]
    live = ((code >> 6) & 1).astype(jnp.float32)
    log_total, deltas, _ = joined(stats_ref[mine_at], stats_ref[code >> 7], sink_ref[...])
    return log_total, deltas, live


def token_side(
    meta_ref, stripes_ref, enc_ref, stats_ref, sink_ref, out_ref, weights_ref, scores_ref
):
    heads = enc_ref.shape[3] // HD
    pairs = heads // 2
    slots = enc_ref.shape[1]
    for slot in range(slots):
        log_total, deltas, live = slot_stats(meta_ref, stats_ref, sink_ref, slot)
        spare = jnp.zeros((8 - 2 * pairs, 2 * CH), jnp.float32)
        columns = jnp.concatenate([log_total, deltas, spare], axis=0).T
        for pair in range(pairs):
            cols = slice(pair * 2 * HD, (pair + 1) * 2 * HD)
            queries = paired(stripes_ref, 0, pair, slot, heads)
            grads = paired(stripes_ref, 1, pair, slot, heads)
            scores = dot(queries, enc_ref[0, slot, :, cols], 1, 1) * SCALE
            d_weights = dot(grads, enc_ref[1, slot, :, cols], 1, 1)
            weights = jnp.exp(scores - columns[:, pair : pair + 1]) * live
            d_scores = weights * (d_weights - columns[:, pairs + pair : pairs + pair + 1]) * SCALE
            weights_ref[slot * pairs + pair] = weights.astype(jnp.bfloat16)
            scores_ref[slot * pairs + pair] = d_scores.astype(jnp.bfloat16)
    for slot in range(slots):
        for pair in range(pairs):
            cols = slice(pair * 2 * HD, (pair + 1) * 2 * HD)
            for which, ref in enumerate((weights_ref, scores_ref)):
                right = enc_ref[1 - which, slot, :, cols]
                rows = dot(ref[slot * pairs + pair], right, 1, 0).astype(jnp.bfloat16)
                for side in range(2):
                    for half in range(2):
                        stripe = (which * heads + 2 * pair + side) * 2 + half
                        at = side * CH + half * HALF
                        out_ref[stripe, slot] = rows[at : at + HALF, side * HD : (side + 1) * HD]


def slot_side(
    meta_ref, stripes_ref, enc_ref, stats_ref, sink_ref, after_ref, *refs
):
    out_ref, weights_ref, scores_ref = refs
    heads = enc_ref.shape[3] // HD
    pairs = heads // 2
    count = out_ref.shape[1]
    first = pl.program_id(0) * count
    for step in range(count):
        slot = first + step
        log_total, deltas, live = slot_stats(meta_ref, stats_ref, sink_ref, slot)
        for pair in range(pairs):
            cols = slice(pair * 2 * HD, (pair + 1) * 2 * HD)
            queries = paired(stripes_ref, 0, pair, slot, heads)
            grads = paired(stripes_ref, 1, pair, slot, heads)
            scores = dot(enc_ref[0, slot, :, cols], queries, 1, 1) * SCALE
            d_weights = dot(enc_ref[1, slot, :, cols], grads, 1, 1)
            weights = jnp.exp(scores - log_total[pair : pair + 1]) * live
            d_scores = weights * (d_weights - deltas[pair : pair + 1]) * SCALE
            weights_ref[step * pairs + pair] = weights.astype(jnp.bfloat16)
            scores_ref[step * pairs + pair] = d_scores.astype(jnp.bfloat16)
    for step in range(count):
        slot = first + step
        for pair in range(pairs):
            cols = slice(pair * 2 * HD, (pair + 1) * 2 * HD)
            for which, ref in enumerate((scores_ref, weights_ref)):
                right = paired(stripes_ref, which, pair, slot, heads)
                rows = dot(ref[step * pairs + pair], right, 1, 0)
                out_ref[which, step, :, cols] = rows.astype(jnp.bfloat16)


def sink_side(meta_ref, stats_ref, sink_ref, after_ref, out_ref, *, spans):
    sink = sink_ref[...]

    def body(span, total):
        here = 2 * span - NB
        live = meta_ref[LIVE, span].astype(jnp.float32)
        left, right = stats_ref[meta_ref[PLACES, here]], stats_ref[meta_ref[PLACES, here + 1]]
        _, deltas, part = joined(left, right, sink)
        return total - part * deltas * live

    out_ref[...] = lax.fori_loop(1, spans, body, jnp.zeros_like(sink), unroll=7)


def route(owner_ref, doc_ref, sink_ref, after_ref, meta_ref, rows_ref):
    f32, i32 = jnp.float32, jnp.int32
    groups, neighs, spans = GROUPS, owner_ref.shape[1], doc_ref.shape[1]

    def ids(shape, dim):
        return lax.broadcasted_iota(i32, shape, dim)

    def one_hot(hits):
        return hits.astype(f32).astype(jnp.bfloat16)

    owner = owner_ref[...]
    in_group = one_hot(ids((groups, neighs), 0) == owner)
    earlier = one_hot(ids((neighs, neighs), 0) < ids((neighs, neighs), 1))
    rank = dot(in_group, earlier, 1, 0) * in_group.astype(f32)
    slot = jnp.sum(rank, axis=0, keepdims=True).astype(i32)
    place = owner * groups + slot
    lane = ids((1, neighs), 1)
    other = jnp.where(lane % 2 == 0, pltpu.roll(place, neighs - 1, 1), pltpu.roll(place, 1, 1))
    reader = lane // NB + 1
    span = ids((1, spans), 1)
    live = ((span >= 1) & (doc_ref[...] == 0)).astype(f32)
    reads = one_hot(ids((spans, neighs), 0) == ids((spans, neighs), 1) // NB + 1)
    read_live = dot(live.astype(jnp.bfloat16), reads, 1, 0)
    low = jnp.minimum(reader, spans - 1).astype(f32) + 64.0 * read_live
    in_slot = one_hot(ids((groups, neighs), 0) == slot)

    def by_slot(row):
        return dot(in_group * row.astype(jnp.bfloat16), in_slot, 1, 1).astype(i32)

    codes = by_slot(low) + 128 * by_slot(other.astype(f32))
    meta_ref[...] = jnp.zeros_like(meta_ref)
    meta_ref[0:groups, 0:groups] = codes
    meta_ref[groups : groups + 1] = place
    meta_ref[groups + 1 : groups + 2, 0:spans] = live.astype(i32)
    left = ids((1, 2 * CH), 1) < CH
    for pair in range(rows_ref.shape[0]):
        rows_ref[pair : pair + 1] = jnp.where(left, sink_ref[2 * pair], sink_ref[2 * pair + 1])


def on_device(queries, encodings, sink, owner, doc_start, d_out):
    seq_count = lax.axis_size("seq")
    tokens, width = queries.shape[1:]
    spans_here = tokens // CH
    heads = width // HD
    pairs = heads // 2
    slots = encodings.shape[2]
    spans = doc_start.shape[1]
    places = seq_count * slots
    bf16 = jnp.bfloat16
    f32 = jnp.float32
    stripe = (HALF, HD)
    flops = 4 * NL * CH * width * slots

    def everywhere(block):
        return lax.all_to_all(block, "seq", split_axis=0, concat_axis=0, tiled=True)

    def call(kernel, name, out, *operands, in_specs=None, out_specs=IN_VMEM, work=0, limit=16, **kw):
        if in_specs is None:
            in_specs = [IN_SMEM if x.dtype == jnp.int32 else IN_VMEM for x in operands]
        return pl.pallas_call(
            kernel,
            in_specs=in_specs,
            out_specs=out_specs,
            out_shape=out,
            compiler_params=pltpu.CompilerParams(vmem_limit_bytes=limit * MIB),
            cost_estimate=pl.CostEstimate(
                flops=work, bytes_accessed=sum(x.nbytes for x in operands), transcendentals=0
            ),
            name=name,
            **kw,
        )(*(in_hbm(x) if spec is IN_HBM else x for x, spec in zip(operands, in_specs)))

    enc = encodings[0]

    def struct(shape, dtype=bf16):
        return jax.ShapeDtypeStruct(shape, dtype)

    def in_hbm(x):
        return pltpu.with_memory_space_constraint(x, pltpu.HBM)

    def by_slots(shape, axis):
        block = tuple(n // STEPS if d == axis else n for d, n in enumerate(shape))
        return pl.BlockSpec(block, lambda i: tuple(i if d == axis else 0 for d in range(len(shape))))

    pairs_of_first = [(2 * i, 2 * (i ^ 2)) for i in range(seq_count)]
    turn = lax.ppermute(sink, ("seq", "dp"), pairs_of_first)
    cut_shape = (2, heads, 2, spans_here) + stripe
    cut, done = call(
        cut_stripes,
        "cut",
        [pltpu.HBM(cut_shape, bf16), struct((8, HD), f32)],
        queries[0],
        d_out[0],
        turn,
        in_specs=[IN_HBM, IN_HBM, IN_VMEM],
        out_specs=[IN_HBM, IN_VMEM],
        scratch_shapes=[
            pltpu.VMEM((2, tokens, width), bf16),
            pltpu.VMEM(cut_shape, bf16),
            pltpu.SemaphoreType.DMA((spans_here,)),
            pltpu.SemaphoreType.DMA((spans_here,)),
        ],
    )
    meta, sink_rows = call(
        route,
        "route",
        [struct((24, HD), jnp.int32), struct((pairs, HD), f32)],
        owner,
        doc_start,
        sink,
        done,
        in_specs=[IN_VMEM, IN_VMEM, IN_SMEM, IN_VMEM],
        out_specs=[IN_VMEM, IN_VMEM],
    )
    all_spans = everywhere(cut.reshape((seq_count, spans_here) + stripe))
    spread = call(
        spread_spans,
        "spread",
        struct((seq_count, slots) + stripe),
        meta,
        all_spans.reshape((spans,) + stripe),
        sink_rows,
    )
    stripes = everywhere(spread)

    stats_shape = (seq_count, slots, heads, HD)
    stats = call(
        stats_of,
        "stats",
        struct(stats_shape, f32),
        stripes,
        enc,
        work=flops,
    )
    all_stats = everywhere(stats).reshape(places, heads, HD)
    whole = (meta, stripes, enc, all_stats, sink_rows)
    partials = call(
        token_side,
        "token_side",
        struct(stripes.shape),
        *whole,
        work=2 * flops,
        scratch_shapes=[pltpu.VMEM((slots * pairs, NL, NL), bf16)] * 2,
    )
    returned = everywhere(partials).reshape((places,) + stripe)
    summed = call(
        add_partials,
        "add_partials",
        pltpu.HBM((spans,) + stripe, bf16),
        meta,
        returned,
    )
    final = everywhere(summed.reshape((seq_count, spans_here) + stripe))
    enc_grads = call(
        slot_side,
        "slot_side",
        struct(enc.shape),
        *whole,
        summed,
        in_specs=[IN_SMEM] + [IN_VMEM] * 4 + [IN_HBM],
        grid=(STEPS,),
        out_specs=by_slots(enc.shape, 1),
        work=2 * flops,
        scratch_shapes=[pltpu.VMEM((slots // STEPS * pairs, NL, NL), bf16)] * 2,
    )
    sink_lanes = call(
        functools.partial(sink_side, spans=spans),
        "sink_side",
        struct((pairs, HD), f32),
        meta,
        all_stats,
        sink_rows,
        summed,
        in_specs=[IN_SMEM, IN_VMEM, IN_VMEM, IN_HBM],
        work=spans * 4096,
    )
    sink_part = jnp.sum(sink_lanes.reshape(heads, CH), axis=1)
    sink_total = sink_part + lax.ppermute(sink_part, "dp", [(0, 1), (1, 0)])

    rows = pl.BlockSpec((tokens, width), lambda: (0, 0))
    attended, grad_query = call(
        join_stripes, "join", [struct((tokens, width))] * 2, final, out_specs=[rows, rows]
    )
    return attended[None], grad_query[None], enc_grads[None], sink_total


def solution(mesh):
    in_specs = (
        P("dp", "seq", "mp"),
        P("dp", None, "seq", None, "mp"),
        P("mp"),
        P("dp", None),
        P("dp", None),
        P("dp", "seq", "mp"),
    )
    out_specs = (
        P("dp", "seq", "mp"),
        P("dp", "seq", "mp"),
        P("dp", None, "seq", None, "mp"),
        P("mp"),
    )
    return jax.shard_map(
        on_device, mesh=mesh, in_specs=in_specs, out_specs=out_specs, check_vma=False
    )
```

```python
import functools

import jax
import jax.numpy as jnp
from jax import lax
from jax.experimental import pallas as pl
from jax.experimental.pallas import tpu as pltpu
from jax.sharding import PartitionSpec as P

HD = 128
CH = 64
NB = 2
NL = 128
HALF = CH // 2
SCALE = HD ** (-0.5)
MIB = 1024 * 1024
STEPS = 2
GROUPS = 16
PLACES, LIVE = GROUPS, GROUPS + 1
IN_VMEM = pl.BlockSpec(memory_space=pltpu.VMEM)
IN_HBM = pl.BlockSpec(memory_space=pltpu.HBM)
IN_SMEM = pl.BlockSpec(memory_space=pltpu.SMEM)


def cut_stripes(query_hbm, grad_hbm, turn_ref, out_hbm, done_ref, *scratch):
    rows_ref, out_ref, in_sems, out_sems = scratch
    done_ref[...] = jnp.zeros_like(done_ref)
    _, heads, halves, spans = out_ref.shape[:4]
    steps = [(which, span) for which in range(2) for span in range(0, spans, 2)]
    loads, stores = [], []
    for step, (which, span) in enumerate(steps):
        rows = pl.ds(span * CH, 2 * CH)
        source = (query_hbm, grad_hbm)[which].at[rows]
        loads.append(pltpu.make_async_copy(source, rows_ref.at[which, rows], in_sems.at[step]))
        loads[step].start()
    for step, (which, first) in enumerate(steps):
        loads[step].wait()
        for head in range(heads):
            for half in range(halves):
                for span in (first, first + 1):
                    row = span * CH + half * HALF
                    out_ref[which, head, half, span] = rows_ref[
                        which, row : row + HALF, head * HD : (head + 1) * HD
                    ]
        at = (which, slice(None), slice(None), pl.ds(first, 2))
        stores.append(pltpu.make_async_copy(out_ref.at[at], out_hbm.at[at], out_sems.at[step]))
        stores[step].start()
    for store in stores:
        store.wait()


def join_stripes(in_ref, attended_hbm, query_hbm, rows_ref, sems):
    spans, heads = in_ref.shape[1], rows_ref.shape[2] // HD
    copies = []
    for which, target in enumerate((attended_hbm, query_hbm)):
        for head in range(heads):
            for half in range(2):
                stripe = (which * heads + head) * 2 + half
                for span in range(spans):
                    row = span * CH + half * HALF
                    rows_ref[which, row : row + HALF, head * HD : (head + 1) * HD] = in_ref[
                        stripe, span
                    ]
        copies.append(pltpu.make_async_copy(rows_ref.at[which], target, sems.at[which]))
        copies[which].start()
    for copy in copies:
        copy.wait()


def spread_spans(meta_ref, in_ref, sink_ref, out_ref):
    for group in range(GROUPS):
        for slot in range(GROUPS):
            out_ref[group, slot] = in_ref[meta_ref[group, slot] & 63]


def add_partials(meta_ref, in_ref, out_hbm, out_ref, sems):
    per_copy = out_ref.shape[0] // sems.shape[0]
    copies = []
    for span in range(out_ref.shape[0]):
        if span == 0:
            out_ref[0] = jnp.zeros(out_ref.shape[1:], jnp.bfloat16)
        else:
            left = in_ref[meta_ref[PLACES, NB * span - 2]].astype(jnp.float32)
            right = in_ref[meta_ref[PLACES, NB * span - 1]].astype(jnp.float32)
            out_ref[span] = (left + right).astype(jnp.bfloat16)
        if span % per_copy == per_copy - 1:
            at = pl.ds(len(copies) * per_copy, per_copy)
            copies.append(
                pltpu.make_async_copy(out_ref.at[at], out_hbm.at[at], sems.at[len(copies)])
            )
            copies[-1].start()
    for copy in copies:
        copy.wait()


def paired(stripes_ref, which, pair, slot, heads):
    nothing = jnp.zeros((CH, HD), jnp.bfloat16)
    blocks = []
    for head in (2 * pair, 2 * pair + 1):
        at = (which * heads + head) * 2
        blocks.append(jnp.concatenate([stripes_ref[at, slot], stripes_ref[at + 1, slot]], axis=0))
    return jnp.concatenate(
        [
            jnp.concatenate([blocks[0], nothing], axis=1),
            jnp.concatenate([nothing, blocks[1]], axis=1),
        ],
        axis=0,
    )


def dot(left, right, left_dim, right_dim):
    return lax.dot_general(
        left, right, (((left_dim,), (right_dim,)), ((), ())), preferred_element_type=jnp.float32
    )


def stats_of(stripes_ref, enc_ref, out_ref):
    heads = enc_ref.shape[3] // HD
    pairs = heads // 2
    for slot in range(out_ref.shape[1]):
        for pair in range(pairs):
            cols = slice(pair * 2 * HD, (pair + 1) * 2 * HD)
            queries = paired(stripes_ref, 0, pair, slot, heads)
            grads = paired(stripes_ref, 1, pair, slot, heads)
            scores = dot(enc_ref[0, slot, :, cols], queries, 1, 1) * SCALE
            d_weights = dot(enc_ref[1, slot, :, cols], grads, 1, 1)
            top = jnp.max(scores, axis=0, keepdims=True)
            powers = jnp.exp(scores - top)
            total = jnp.sum(powers, axis=0, keepdims=True)
            out_ref[0, slot, pair : pair + 1] = top + jnp.log(total)
            delta = jnp.sum(powers * d_weights, axis=0, keepdims=True) / total
            out_ref[0, slot, pairs + pair : pairs + pair + 1] = delta
    for dest in range(1, out_ref.shape[0]):
        out_ref[dest] = out_ref[0]


def joined(mine, other, sink):
    pairs = sink.shape[0]
    log_a, log_b = mine[:pairs], other[:pairs]
    top = jnp.maximum(jnp.maximum(log_a, log_b), sink)
    part_a, part_b, part_s = jnp.exp(log_a - top), jnp.exp(log_b - top), jnp.exp(sink - top)
    total = part_a + part_b + part_s
    deltas = (part_a * mine[pairs:] + part_b * other[pairs:]) / total
    return top + jnp.log(total), deltas, part_s / total


def slot_stats(meta_ref, stats_ref, sink_ref, slot):
    group = lax.axis_index("seq")
    mine_at = group * GROUPS + slot
    code = meta_ref[group, slot]
    live = ((code >> 6) & 1).astype(jnp.float32)
    log_total, deltas, _ = joined(stats_ref[mine_at], stats_ref[code >> 7], sink_ref[...])
    return log_total, deltas, live


def token_side(
    meta_ref, stripes_ref, enc_ref, stats_ref, sink_ref, out_ref, weights_ref, scores_ref
):
    heads = enc_ref.shape[3] // HD
    pairs = heads // 2
    slots = enc_ref.shape[1]
    for slot in range(slots):
        log_total, deltas, live = slot_stats(meta_ref, stats_ref, sink_ref, slot)
        spare = jnp.zeros((8 - 2 * pairs, 2 * CH), jnp.float32)
        columns = jnp.concatenate([log_total, deltas, spare], axis=0).T
        for pair in range(pairs):
            cols = slice(pair * 2 * HD, (pair + 1) * 2 * HD)
            queries = paired(stripes_ref, 0, pair, slot, heads)
            grads = paired(stripes_ref, 1, pair, slot, heads)
            scores = dot(queries, enc_ref[0, slot, :, cols], 1, 1) * SCALE
            d_weights = dot(grads, enc_ref[1, slot, :, cols], 1, 1)
            weights = jnp.exp(scores - columns[:, pair : pair + 1]) * live
            d_scores = weights * (d_weights - columns[:, pairs + pair : pairs + pair + 1]) * SCALE
            weights_ref[slot * pairs + pair] = weights.astype(jnp.bfloat16)
            scores_ref[slot * pairs + pair] = d_scores.astype(jnp.bfloat16)
    for slot in range(slots):
        for pair in range(pairs):
            cols = slice(pair * 2 * HD, (pair + 1) * 2 * HD)
            for which, ref in enumerate((weights_ref, scores_ref)):
                right = enc_ref[1 - which, slot, :, cols]
                rows = dot(ref[slot * pairs + pair], right, 1, 0).astype(jnp.bfloat16)
                for side in range(2):
                    for half in range(2):
                        stripe = (which * heads + 2 * pair + side) * 2 + half
                        at = side * CH + half * HALF
                        out_ref[stripe, slot] = rows[at : at + HALF, side * HD : (side + 1) * HD]


def slot_side(
    meta_ref, stripes_ref, enc_ref, stats_ref, sink_ref, after_ref, *refs
):
    out_ref, weights_ref, scores_ref = refs
    heads = enc_ref.shape[3] // HD
    pairs = heads // 2
    count = out_ref.shape[1]
    first = pl.program_id(0) * count
    for step in range(count):
        slot = first + step
        log_total, deltas, live = slot_stats(meta_ref, stats_ref, sink_ref, slot)
        for pair in range(pairs):
            cols = slice(pair * 2 * HD, (pair + 1) * 2 * HD)
            queries = paired(stripes_ref, 0, pair, slot, heads)
            grads = paired(stripes_ref, 1, pair, slot, heads)
            scores = dot(enc_ref[0, slot, :, cols], queries, 1, 1) * SCALE
            d_weights = dot(enc_ref[1, slot, :, cols], grads, 1, 1)
            weights = jnp.exp(scores - log_total[pair : pair + 1]) * live
            d_scores = weights * (d_weights - deltas[pair : pair + 1]) * SCALE
            weights_ref[step * pairs + pair] = weights.astype(jnp.bfloat16)
            scores_ref[step * pairs + pair] = d_scores.astype(jnp.bfloat16)
    for step in range(count):
        slot = first + step
        for pair in range(pairs):
            cols = slice(pair * 2 * HD, (pair + 1) * 2 * HD)
            for which, ref in enumerate((scores_ref, weights_ref)):
                right = paired(stripes_ref, which, pair, slot, heads)
                rows = dot(ref[step * pairs + pair], right, 1, 0)
                out_ref[which, step, :, cols] = rows.astype(jnp.bfloat16)


def sink_side(meta_ref, stats_ref, sink_ref, after_ref, out_ref, *, spans):
    sink = sink_ref[...]

    def body(span, total):
        here = 2 * span - NB
        live = meta_ref[LIVE, span].astype(jnp.float32)
        left, right = stats_ref[meta_ref[PLACES, here]], stats_ref[meta_ref[PLACES, here + 1]]
        _, deltas, part = joined(left, right, sink)
        return total - part * deltas * live

    out_ref[...] = lax.fori_loop(1, spans, body, jnp.zeros_like(sink), unroll=7)


def route(owner_ref, doc_ref, sink_ref, after_ref, meta_ref, rows_ref):
    f32, i32 = jnp.float32, jnp.int32
    groups, neighs, spans = GROUPS, owner_ref.shape[1], doc_ref.shape[1]

    def ids(shape, dim):
        return lax.broadcasted_iota(i32, shape, dim)

    def one_hot(hits):
        return hits.astype(f32).astype(jnp.bfloat16)

    owner = owner_ref[...]
    in_group = one_hot(ids((groups, neighs), 0) == owner)
    earlier = one_hot(ids((neighs, neighs), 0) < ids((neighs, neighs), 1))
    rank = dot(in_group, earlier, 1, 0) * in_group.astype(f32)
    slot = jnp.sum(rank, axis=0, keepdims=True).astype(i32)
    place = owner * groups + slot
    lane = ids((1, neighs), 1)
    other = jnp.where(lane % 2 == 0, pltpu.roll(place, neighs - 1, 1), pltpu.roll(place, 1, 1))
    reader = lane // NB + 1
    span = ids((1, spans), 1)
    live = ((span >= 1) & (doc_ref[...] == 0)).astype(f32)
    reads = one_hot(ids((spans, neighs), 0) == ids((spans, neighs), 1) // NB + 1)
    read_live = dot(live.astype(jnp.bfloat16), reads, 1, 0)
    low = jnp.minimum(reader, spans - 1).astype(f32) + 64.0 * read_live
    in_slot = one_hot(ids((groups, neighs), 0) == slot)

    def by_slot(row):
        return dot(in_group * row.astype(jnp.bfloat16), in_slot, 1, 1).astype(i32)

    codes = by_slot(low) + 128 * by_slot(other.astype(f32))
    meta_ref[...] = jnp.zeros_like(meta_ref)
    meta_ref[0:groups, 0:groups] = codes
    meta_ref[groups : groups + 1] = place
    meta_ref[groups + 1 : groups + 2, 0:spans] = live.astype(i32)
    left = ids((1, 2 * CH), 1) < CH
    for pair in range(rows_ref.shape[0]):
        rows_ref[pair : pair + 1] = jnp.where(left, sink_ref[2 * pair], sink_ref[2 * pair + 1])


def on_device(queries, encodings, sink, owner, doc_start, d_out):
    seq_count = lax.axis_size("seq")
    tokens, width = queries.shape[1:]
    spans_here = tokens // CH
    heads = width // HD
    pairs = heads // 2
    slots = encodings.shape[2]
    spans = doc_start.shape[1]
    places = seq_count * slots
    bf16 = jnp.bfloat16
    f32 = jnp.float32
    stripe = (HALF, HD)
    flops = 4 * NL * CH * width * slots

    def everywhere(block):
        return lax.all_to_all(block, "seq", split_axis=0, concat_axis=0, tiled=True)

    def call(kernel, name, out, *operands, in_specs=None, out_specs=IN_VMEM, work=0, limit=16, **kw):
        if in_specs is None:
            in_specs = [IN_SMEM if x.dtype == jnp.int32 else IN_VMEM for x in operands]
        return pl.pallas_call(
            kernel,
            in_specs=in_specs,
            out_specs=out_specs,
            out_shape=out,
            compiler_params=pltpu.CompilerParams(vmem_limit_bytes=limit * MIB),
            cost_estimate=pl.CostEstimate(
                flops=work, bytes_accessed=sum(x.nbytes for x in operands), transcendentals=0
            ),
            name=name,
            **kw,
        )(*(in_hbm(x) if spec is IN_HBM else x for x, spec in zip(operands, in_specs)))

    enc = encodings[0]

    def struct(shape, dtype=bf16):
        return jax.ShapeDtypeStruct(shape, dtype)

    def in_hbm(x):
        return pltpu.with_memory_space_constraint(x, pltpu.HBM)

    def by_slots(shape, axis):
        block = tuple(n // STEPS if d == axis else n for d, n in enumerate(shape))
        return pl.BlockSpec(block, lambda i: tuple(i if d == axis else 0 for d in range(len(shape))))

    pairs_of_first = [(2 * i, 2 * (i ^ 2)) for i in range(seq_count)]
    turn = lax.ppermute(sink, ("seq", "dp"), pairs_of_first)
    cut_shape = (2, heads, 2, spans_here) + stripe
    cut, done = call(
        cut_stripes,
        "cut",
        [pltpu.HBM(cut_shape, bf16), struct((8, HD), f32)],
        queries[0],
        d_out[0],
        turn,
        in_specs=[IN_HBM, IN_HBM, IN_VMEM],
        out_specs=[IN_HBM, IN_VMEM],
        scratch_shapes=[
            pltpu.VMEM((2, tokens, width), bf16),
            pltpu.VMEM(cut_shape, bf16),
            pltpu.SemaphoreType.DMA((spans_here,)),
            pltpu.SemaphoreType.DMA((spans_here,)),
        ],
    )
    meta, sink_rows = call(
        route,
        "route",
        [struct((24, HD), jnp.int32), struct((pairs, HD), f32)],
        owner,
        doc_start,
        sink,
        done,
        in_specs=[IN_VMEM, IN_VMEM, IN_SMEM, IN_VMEM],
        out_specs=[IN_VMEM, IN_VMEM],
    )
    all_spans = everywhere(cut.reshape((seq_count, spans_here) + stripe))
    spread = call(
        spread_spans,
        "spread",
        struct((seq_count, slots) + stripe),
        meta,
        all_spans.reshape((spans,) + stripe),
        sink_rows,
    )
    stripes = everywhere(spread)

    stats_shape = (seq_count, slots, heads, HD)
    stats = call(
        stats_of,
        "stats",
        struct(stats_shape, f32),
        stripes,
        enc,
        work=flops,
    )
    all_stats = everywhere(stats).reshape(places, heads, HD)
    whole = (meta, stripes, enc, all_stats, sink_rows)
    partials = call(
        token_side,
        "token_side",
        struct(stripes.shape),
        *whole,
        work=2 * flops,
        scratch_shapes=[pltpu.VMEM((slots * pairs, NL, NL), bf16)] * 2,
    )
    returned = everywhere(partials).reshape((places,) + stripe)
    summed = call(
        add_partials,
        "add_partials",
        pltpu.HBM((spans,) + stripe, bf16),
        meta,
        returned,
        out_specs=IN_HBM,
        scratch_shapes=[pltpu.VMEM((spans,) + stripe, bf16), pltpu.SemaphoreType.DMA((4,))],
    )
    final = everywhere(summed.reshape((seq_count, spans_here) + stripe))
    enc_grads = call(
        slot_side,
        "slot_side",
        struct(enc.shape),
        *whole,
        summed,
        in_specs=[IN_SMEM] + [IN_VMEM] * 4 + [IN_HBM],
        grid=(STEPS,),
        out_specs=by_slots(enc.shape, 1),
        work=2 * flops,
        scratch_shapes=[pltpu.VMEM((slots // STEPS * pairs, NL, NL), bf16)] * 2,
    )
    sink_lanes = call(
        functools.partial(sink_side, spans=spans),
        "sink_side",
        struct((pairs, HD), f32),
        meta,
        all_stats,
        sink_rows,
        summed,
        in_specs=[IN_SMEM, IN_VMEM, IN_VMEM, IN_HBM],
        work=spans * 4096,
    )
    sink_part = jnp.sum(sink_lanes.reshape(heads, CH), axis=1)
    sink_total = sink_part + lax.ppermute(sink_part, "dp", [(0, 1), (1, 0)])

    attended, grad_query = call(
        join_stripes,
        "join",
        [pltpu.HBM((tokens, width), bf16)] * 2,
        final,
        out_specs=[IN_HBM, IN_HBM],
        scratch_shapes=[pltpu.VMEM((2, tokens, width), bf16), pltpu.SemaphoreType.DMA((2,))],
    )
    return attended[None], grad_query[None], enc_grads[None], sink_total


def solution(mesh):
    in_specs = (
        P("dp", "seq", "mp"),
        P("dp", None, "seq", None, "mp"),
        P("mp"),
        P("dp", None),
        P("dp", None),
        P("dp", "seq", "mp"),
    )
    out_specs = (
        P("dp", "seq", "mp"),
        P("dp", "seq", "mp"),
        P("dp", None, "seq", None, "mp"),
        P("mp"),
    )
    return jax.shard_map(
        on_device, mesh=mesh, in_specs=in_specs, out_specs=out_specs, check_vma=False
    )
```
